512 devices in a mesh: row: 4 (over x), col: 16 (over z_hi, y), depth: 8 (over z_lo, core).
Axes of the slice: x: 4, y: 4, z: 16 (z_hi: 4, z_lo: 4; z = z_hi * 4 + z_lo), core: 2. Of those that a mesh axis runs over, the one named last changes fastest.
Arguments:
- integrals: bfloat16 [800, 800, 512], P('col', 'depth', 'row'), may hold values from -0.15625 to 0.15625
- amplitudes: bfloat16 [16, 800, 3200], P('col', ('depth', 'row')), may hold values from -6 to 6
- a_offsets: int32 [9], replicated, may hold values from 0 to 32, as said below
- vir_offsets: int32 [9], replicated, may hold values from 0 to 800, as said below
- c_offsets: int32 [9], replicated, may hold values from 0 to 16, as said below
Outputs:
- ladder: bfloat16 [32, 800, 3200], P(('row', 'depth'), 'col')
The draws below stay inside these ranges and needn't reach their ends.
Inputs may be any that keep to these rules, and one draw needn't show every extreme that they name: `a_offsets`: offsets of the 8 irrep blocks of the a orbitals: the first is 0, the last is 32, non-decreasing; block k holds irrep k and has at least one orbital. `vir_offsets`: offsets of the 8 irrep blocks of the virtual orbitals: the first is 0, the last is 800, non-decreasing; block k holds irrep k and has at least one orbital. `c_offsets`: offsets of the 8 irrep blocks of the slab's c orbitals: the first is 0, the last is 16, non-decreasing; block k holds irrep k and has at least one orbital.
All inputs are finite; a program needn't handle non-finite values.
Results may differ from the reference program's by a relative error of at most 0.017.
Values may be sent and summed in bfloat16 or wider, within the bound.
No kernel may reach another device: no remote copies, remote signals or barrier semaphores. Data moves between devices by JAX's collectives and lax.ppermute only.
A program may use at most 64 MiB of HBM per device.

```python
import jax
import jax.numpy as jnp

NV = 800
NO = 100
CB = 16
I = 32
A = 32
N_DEPTH = 8


def block_offsets(key, count):
    spread = max(1, count // 32)
    first_half = jax.random.randint(key, (4,), -spread, spread + 1, dtype=jnp.int32)
    mirror = jax.random.permutation(jax.random.fold_in(key, 1), 4)
    deltas = jnp.concatenate([first_half, -first_half[mirror]])
    order = jax.random.permutation(jax.random.fold_in(key, 2), 8)
    widths = (count // 8 + deltas[order]).astype(jnp.int32)
    return jnp.concatenate([jnp.zeros((1,), jnp.int32), jnp.cumsum(widths).astype(jnp.int32)])


def draw_a_offsets(key, part):
    key = jax.random.fold_in(key, 11)
    return block_offsets(key, A)


def draw_vir_offsets(key, part):
    key = jax.random.fold_in(key, 23)
    return block_offsets(key, NV)


def draw_c_offsets(key, part):
    key = jax.random.fold_in(key, 37)
    return block_offsets(key, CB)


def level_of(rng, extent, pieces, low, top_value):
    factor_of, own = 1.0, jax.random.fold_in(rng, 6)
    for position, blocks in pieces:
        heights = jnp.exp(jax.random.uniform(jax.random.fold_in(own, position), (blocks,), jnp.float32, low / len(pieces), top_value / len(pieces)))
        factor_of = factor_of * jnp.repeat(heights, extent[position] // blocks).reshape([-1 if axis == position else 1 for axis in range(len(extent))])
    return factor_of


def gaussian(key, extent, width, most, pieces=(), kind=jnp.bfloat16):
    drawn = width * jax.random.normal(key, extent, jnp.float32)
    if pieces:
        drawn = drawn * level_of(key, extent, pieces, -0.22, 0.18)
    return jnp.clip(drawn, -most, most).astype(kind)


def setup_inputs(seed: int = 0) -> dict:
    seeds = jax.random.split(jax.random.key(seed), 6)
    return {
        "integrals": gaussian(seeds[0], (NV, NV, A * CB), (CB * NV // 8) ** -0.5, 0.15625, ((0, 16), (1, 8), (2, 4))),
        "amplitudes": gaussian(seeds[1], (CB, NV, I * NO), 1.0, 6.0, ((0, 16), (1, 32))),
        "a_offsets": draw_a_offsets(jax.random.fold_in(seeds[5], 71), 0),
        "vir_offsets": draw_vir_offsets(jax.random.fold_in(seeds[5], 71), 0),
        "c_offsets": draw_c_offsets(jax.random.fold_in(seeds[5], 71), 0),
    }


def labels_of(offsets, count):
    index = jnp.arange(count, dtype=jnp.int32)
    above = (index[:, None] >= offsets[None, 1:8]).astype(jnp.int32)
    return jnp.sum(above, axis=1).astype(jnp.int32)


def reference(integrals, amplitudes, a_offsets, vir_offsets, c_offsets):
    a_irrep = labels_of(a_offsets, A)
    vir_irrep = labels_of(vir_offsets, NV)
    c_irrep = labels_of(c_offsets, CB)
    d_block = NV // N_DEPTH
    four = integrals.reshape(NV, NV, A, CB)
    running = jnp.zeros((A * NV, I * NO), jnp.float32)
    for block_index in range(N_DEPTH):
        lower = block_index * d_block
        d_labels = vir_irrep[lower:lower + d_block]
        product = jnp.bitwise_xor(
            jnp.bitwise_xor(a_irrep[:, None, None, None], vir_irrep[None, :, None, None]),
            jnp.bitwise_xor(c_irrep[None, None, :, None], d_labels[None, None, None, :]))
        int_block = four[:, lower:lower + d_block, :, :].transpose(2, 0, 3, 1)
        masked = jnp.where(product == 0, int_block, jnp.zeros_like(int_block))
        amp_block = amplitudes[:, lower:lower + d_block, :]
        partial_sum = jnp.dot(masked.reshape(A * NV, CB * d_block),
                              amp_block.reshape(CB * d_block, I * NO),
                              preferred_element_type=jnp.float32).astype(jnp.bfloat16)
        running = running + partial_sum.astype(jnp.float32)
    return running.reshape(A, NV, I * NO).astype(jnp.bfloat16)
```

```python
import jax
import jax.numpy as jnp
from jax import lax
from jax.experimental import pallas as pl
from jax.experimental.pallas import tpu as pltpu
from jax.sharding import Mesh, PartitionSpec as P

CB = 16
A_ROW = 8
B_DEV = 50
D_DEV = 100
RANKS = 9
N_DEV = 800
ROWS = A_ROW * B_DEV
KB = 128


def count_at_or_above(index, offsets):
    total = jnp.zeros_like(index)
    for k in range(1, 8):
        total = total + jnp.where(index >= offsets[k], 1, 0)
    return total


def squeeze_kernel(place, a_off, v_off, c_off, v_ref, w_ref, by_b):
    step = pl.program_id(0)
    b_step = v_ref.shape[0]
    lane = lax.broadcasted_iota(jnp.int32, (D_DEV, KB), 1)
    drow = lax.broadcasted_iota(jnp.int32, (D_DEV, KB), 0)
    base = count_at_or_above(drow + place[1], v_off)
    base = base ^ count_at_or_above((lane >> 4) + place[2], a_off)
    base = base ^ count_at_or_above(lane & 15, c_off)
    elane = lax.broadcasted_iota(jnp.int32, (RANKS * A_ROW, KB), 1)
    erow = lax.broadcasted_iota(jnp.int32, (RANKS * A_ROW, KB), 0)
    c = elane & 15
    c_label = count_at_or_above(c, c_off)
    first = jnp.zeros_like(c)
    for k in range(8):
        first = first + jnp.where(c_label == k, c_off[k], 0)
    pick = ((elane >> 4) == (erow & 7)) & ((c - first) == (erow >> 3))
    pick = jnp.where(pick, 1.0, 0.0).astype(jnp.bfloat16)

    @pl.when(step == 0)
    def _():
        by_b[...] = jnp.zeros_like(by_b)

    b0 = place[0] + step * b_step
    for p in range(b_step // 2):
        halves = []
        for q in range(2):
            b = 2 * p + q
            b_label = count_at_or_above(b0 + b, v_off)
            x = jnp.where(base == b_label, v_ref[b].astype(jnp.float32), 0.0).astype(jnp.bfloat16)
            halves.append(lax.dot_general(pick, x, (((1,), (1,)), ((), ())), preferred_element_type=jnp.float32))
        for r in range(RANKS):
            pair = jnp.concatenate([h[r * A_ROW:(r + 1) * A_ROW] for h in halves], axis=0)
            start = pl.multiple_of(step * (b_step * A_ROW) + 16 * p, 16)
            by_b[r, pl.ds(start, 16), pl.ds(0, D_DEV)] = pair.astype(jnp.bfloat16)

    @pl.when(step == pl.num_programs(0) - 1)
    def _():
        to = lax.broadcasted_iota(jnp.int32, (ROWS, ROWS), 0)
        source = lax.broadcasted_iota(jnp.int32, (ROWS, ROWS), 1)
        a = jnp.zeros_like(to)
        for k in range(1, A_ROW):
            a = a + jnp.where(to >= k * B_DEV, 1, 0)
        move = jnp.where(source == (to - a * B_DEV) * A_ROW + a, 1.0, 0.0).astype(jnp.bfloat16)
        for r in range(RANKS):
            w_ref[r] = jnp.dot(move, by_b[r], preferred_element_type=jnp.float32).astype(jnp.bfloat16)


def squeeze(place, a_off, v_off, c_off, v):
    b_step = 10
    smem = pl.BlockSpec(memory_space=pltpu.SMEM)
    return pl.pallas_call(
        squeeze_kernel,
        grid=(B_DEV // b_step,),
        in_specs=[smem] * 4 + [pl.BlockSpec((b_step, D_DEV, KB), lambda i: (i, 0, 0))],
        out_specs=pl.BlockSpec((RANKS, ROWS, KB), lambda i: (0, 0, 0)),
        out_shape=jax.ShapeDtypeStruct((RANKS, ROWS, KB), jnp.bfloat16),
        scratch_shapes=[pltpu.VMEM((RANKS, ROWS, KB), jnp.bfloat16)],
        compiler_params=pltpu.CompilerParams(vmem_limit_bytes=40 * 2**20),
        cost_estimate=pl.CostEstimate(flops=2 * 5000 * 128 * 72, bytes_accessed=2400000, transcendentals=0),
        name="squeeze",
    )(place, a_off, v_off, c_off, v)


def contract_kernel(place, a_off, v_off, c_off, w_ref, t0, t1, t2, t3, mine_ref, other_ref, tp, lhs, acc, result):
    step = pl.program_id(0)

    @pl.when(step == 0)
    def _():
        tp[...] = jnp.zeros_like(tp)
        for j, t in enumerate((t0, t1, t2, t3)):
            for z in range(4):
                tp[pl.ds((4 * j + z) * KB, D_DEV), :] = t[z]

    row = lax.broadcasted_iota(jnp.int32, (ROWS, KB), 0)
    lane = lax.broadcasted_iota(jnp.int32, (ROWS, KB), 1)
    a = jnp.zeros_like(row)
    for k in range(1, A_ROW):
        a = a + jnp.where(row >= k * B_DEV, 1, 0)
    base = count_at_or_above(row - a * B_DEV + place[0], v_off)
    base = base ^ count_at_or_above(a + step * A_ROW, a_off)
    base = base ^ count_at_or_above(lane + place[1], v_off)
    for j in range(4):
        y = (place[3] + j) & 3
        for z in range(4):
            c = 4 * z + y
            c_label = count_at_or_above(c, c_off)
            rank = c - c_off[c_label]
            w = w_ref[0, rank].astype(jnp.float32)
            lhs[:, pl.ds((4 * j + z) * KB, KB)] = jnp.where(base == c_label, w, 0.0).astype(jnp.bfloat16)
    acc[...] = jnp.dot(lhs[...], tp[...], preferred_element_type=jnp.float32)
    for s in range(4):
        @pl.when(step == s)
        def _():
            for a in range(A_ROW):
                result[a, pl.ds(s * B_DEV, B_DEV), :] = acc[pl.ds(a * B_DEV, B_DEV), :]

    @pl.when(step == 3)
    def _():
        for z in range(4):
            low = result[2 * z].astype(jnp.bfloat16)
            high = result[2 * z + 1].astype(jnp.bfloat16)
            is_low = place[4] == 0
            mine_ref[z] = jnp.where(is_low, low, high)
            other_ref[z] = jnp.where(is_low, high, low)


def contract(place, a_off, v_off, c_off, w, ts):
    smem = pl.BlockSpec(memory_space=pltpu.SMEM)
    t_spec = pl.BlockSpec((4, D_DEV, N_DEV), lambda i: (0, 0, 0))
    o_spec = pl.BlockSpec((4, 4 * B_DEV, N_DEV), lambda i: (0, 0, 0))
    o_shape = jax.ShapeDtypeStruct((4, 4 * B_DEV, N_DEV), jnp.bfloat16)
    return pl.pallas_call(
        contract_kernel,
        grid=(4,),
        in_specs=[smem] * 4 + [pl.BlockSpec((1, RANKS, ROWS, KB), lambda i: (i, 0, 0, 0))] + [t_spec] * 4,
        out_specs=[o_spec, o_spec],
        out_shape=[o_shape, o_shape],
        scratch_shapes=[
            pltpu.VMEM((CB * KB, N_DEV), jnp.bfloat16),
            pltpu.VMEM((ROWS, CB * KB), jnp.bfloat16),
            pltpu.VMEM((ROWS, N_DEV), jnp.float32),
            pltpu.VMEM((A_ROW, 4 * B_DEV, N_DEV), jnp.float32),
        ],
        compiler_params=pltpu.CompilerParams(vmem_limit_bytes=50 * 2**20),
        cost_estimate=pl.CostEstimate(flops=2 * 1600 * 2048 * 800, bytes_accessed=10000000, transcendentals=0),
        name="contract",
    )(place, a_off, v_off, c_off, w, *ts)


def turn(k):
    return [(i, (i + k) % 4) for i in range(4)]


def shards(integrals, amplitudes, a_offsets, vir_offsets, c_offsets):
    zh, y, x = lax.axis_index("zh"), lax.axis_index("y"), lax.axis_index("x")
    zl, core = lax.axis_index("zl"), lax.axis_index("core")
    place = jnp.stack([(zh * 4 + y) * B_DEV, (zl * 2 + core) * D_DEV, x * A_ROW, y, core]).astype(jnp.int32)
    offs = (a_offsets, vir_offsets, c_offsets)
    t = lax.all_to_all(amplitudes.reshape(25, 4, N_DEV), "x", 1, 0, tiled=True).reshape(1, D_DEV, N_DEV)
    w = squeeze(place, *offs, integrals)
    w = lax.all_gather(w, "x", axis=0)
    t = lax.all_gather(t, "zh", axis=0, tiled=True)
    t1, t2, t3 = (lax.ppermute(t, "y", turn(k)) for k in (3, 2, 1))
    mine, other = contract(place, *offs, w, (t, t1, t2, t3))
    got = lax.ppermute(other, "core", [(0, 1), (1, 0)])

    def pair(k):
        which = zl ^ k
        a = lax.dynamic_index_in_dim(mine, which, 0, keepdims=False).astype(jnp.float32)
        b = lax.dynamic_index_in_dim(got, which, 0, keepdims=False).astype(jnp.float32)
        return a + b

    total = pair(0)
    for part in [lax.ppermute(pair(k).astype(jnp.bfloat16), "zl", [(i, i ^ k) for i in range(4)]) for k in (3, 2, 1)]:
        total = total + part.astype(jnp.float32)
    out = lax.all_to_all(total.astype(jnp.bfloat16).reshape(4, B_DEV, N_DEV), "x", 0, 0, tiled=True)
    return out.transpose(1, 0, 2).reshape(1, B_DEV, 4 * N_DEV)


def solution(mesh):
    fine = Mesh(mesh.devices.reshape(4, 4, 4, 4, 2), ("x", "zh", "y", "zl", "core"))
    in_specs = (P(("zh", "y"), ("zl", "core"), "x"), P(("zh", "y"), ("zl", "core", "x"), None), P(), P(), P())
    out_specs = P(("x", "zl", "core"), ("zh", "y"), None)
    return jax.shard_map(shards, mesh=fine, in_specs=in_specs, out_specs=out_specs, check_vma=False)
```

```python
import functools

import jax
import jax.numpy as jnp
from jax import lax
from jax.experimental import pallas as pl
from jax.experimental.pallas import tpu as pltpu
from jax.sharding import Mesh, PartitionSpec as P

CB = 16
A_ROW = 8
B_DEV = 50
D_DEV = 100
N_DEV = 400
GROUPS = 8
ROWS = A_ROW * B_DEV
KB = 128
TILES = N_DEV // KB
LEFT = N_DEV - TILES * KB
PACKED = 160
SWAP = [(0, 1), (1, 0)]
RANKS_MOST = 9
RANKS_FEW = 3


def count_at_or_above(index, offsets):
    total = jnp.zeros_like(index)
    for k in range(1, 8):
        total = total + jnp.where(index >= offsets[k], 1, 0)
    return total


class Part:
    def __init__(self, table, start):
        self.table, self.start = table, start

    def __getitem__(self, k):
        return self.table[self.start + k]


def parts_of(table):
    return Part(table, 0), Part(table, 8), Part(table, 17), Part(table, 26)


def a_of(row):
    a = jnp.zeros_like(row)
    for k in range(1, A_ROW):
        a = a + jnp.where(row >= k * B_DEV, 1, 0)
    return a


def squeeze_kernel(ranks, table, v_ref, w_ref, by_b):
    place, a_off, v_off, c_off = parts_of(table)
    step = pl.program_id(0)
    b_step = v_ref.shape[0]
    lane = lax.broadcasted_iota(jnp.int32, (D_DEV, KB), 1)
    drow = lax.broadcasted_iota(jnp.int32, (D_DEV, KB), 0)
    base = count_at_or_above(drow + place[1], v_off)
    base = base ^ count_at_or_above((lane >> 4) + place[2] * A_ROW, a_off)
    base = base ^ count_at_or_above(lane & 15, c_off)
    elane = lax.broadcasted_iota(jnp.int32, (ranks * A_ROW, KB), 1)
    erow = lax.broadcasted_iota(jnp.int32, (ranks * A_ROW, KB), 0)
    c = elane & 15
    c_label = count_at_or_above(c, c_off)
    first = jnp.zeros_like(c)
    for k in range(8):
        first = first + jnp.where(c_label == k, c_off[k], 0)
    pick = ((elane >> 4) == (erow & 7)) & ((c - first) == (erow >> 3))
    pick = jnp.where(pick, 1.0, 0.0).astype(jnp.bfloat16)

    @pl.when(step == 0)
    def _():
        by_b[...] = jnp.zeros_like(by_b)

    b0 = place[0] + place[5] * B_DEV + step * b_step
    for p in range(b_step // 2):
        halves = []
        for q in range(2):
            b = 2 * p + q
            b_label = count_at_or_above(b0 + b, v_off)
            x = jnp.where(base == b_label, v_ref[b].astype(jnp.float32), 0.0).astype(jnp.bfloat16)
            halves.append(lax.dot_general(pick, x, (((1,), (1,)), ((), ())), preferred_element_type=jnp.float32))
        for r in range(ranks):
            pair = jnp.concatenate([h[r * A_ROW:(r + 1) * A_ROW] for h in halves], axis=0)
            start = pl.multiple_of(step * (b_step * A_ROW) + 16 * p, 16)
            by_b[r, pl.ds(start, 16), pl.ds(0, D_DEV)] = pair.astype(jnp.bfloat16)

    @pl.when(step == pl.num_programs(0) - 1)
    def _():
        to = lax.broadcasted_iota(jnp.int32, (ROWS, ROWS), 0)
        source = lax.broadcasted_iota(jnp.int32, (ROWS, ROWS), 1)
        a = a_of(to)
        move = jnp.where(source == (to - a * B_DEV) * A_ROW + a, 1.0, 0.0).astype(jnp.bfloat16)
        for r in range(ranks):
            w_ref[r] = jnp.dot(move, by_b[r], preferred_element_type=jnp.float32).astype(jnp.bfloat16)


SMEM = pl.BlockSpec(memory_space=pltpu.SMEM)


def squeeze(ranks, table, v):
    b_step = 10
    return pl.pallas_call(
        functools.partial(squeeze_kernel, ranks),
        grid=(B_DEV // b_step,),
        in_specs=[SMEM, pl.BlockSpec((b_step, D_DEV, KB), lambda i: (i, 0, 0))],
        out_specs=pl.BlockSpec((ranks, ROWS, KB), lambda i: (0, 0, 0)),
        out_shape=jax.ShapeDtypeStruct((ranks, ROWS, KB), jnp.bfloat16),
        scratch_shapes=[pltpu.VMEM((ranks, ROWS, KB), jnp.bfloat16)],
        compiler_params=pltpu.CompilerParams(vmem_limit_bytes=40 * 2**20),
        cost_estimate=pl.CostEstimate(flops=2 * 5000 * 128 * 8 * ranks, bytes_accessed=2400000, transcendentals=0),
        name="squeeze",
    )(table, v)


def contract_kernel(table, w_ref, t0, t1, mine_ref, other_ref, tp, a_labels, bd_labels, tail, packed):
    place, a_off, v_off, c_off = parts_of(table)
    step = pl.program_id(0)

    @pl.when(step == 0)
    def _():
        tp[...] = jnp.zeros_like(tp)
        tail[...] = jnp.zeros_like(tail)
        packed[...] = jnp.zeros_like(packed)
        for j, t in enumerate((t0, t1)):
            for z in range(4):
                block = t[z].astype(jnp.float32)
                for h in range(2):
                    part = block[:, h * N_DEV:(h + 1) * N_DEV].astype(jnp.bfloat16)
                    tp[pl.ds((8 * j + 2 * z + h) * KB, D_DEV), :] = part
        row = lax.broadcasted_iota(jnp.int32, (ROWS, KB), 0)
        lane = lax.broadcasted_iota(jnp.int32, (ROWS, KB), 1)
        a = a_of(row)
        d_label = count_at_or_above(lane + place[1], v_off)
        for s in range(4):
            a_labels[s] = count_at_or_above(a + s * A_ROW, a_off)
        for s in range(2):
            bd_labels[s] = d_label ^ count_at_or_above(row - a * B_DEV + place[0] + s * 2 * B_DEV, v_off)

    base = (a_labels[step >> 1] ^ bd_labels[step & 1]).astype(jnp.float32).astype(jnp.bfloat16)
    acc = None
    for j in range(2):
        for z in range(0, 4, 2):
            masked = []
            for i in range(4):
                c = 4 * (z + i // 2) + 2 * (i % 2) + (place[3] ^ j)
                c_label = count_at_or_above(c, c_off)
                rank = jnp.minimum(c - c_off[c_label], w_ref.shape[2] - 1)
                w = w_ref[0, 0, rank]
                hit = base == c_label.astype(jnp.float32).astype(jnp.bfloat16)
                masked.append(jnp.where(hit, w, jnp.zeros_like(w)))
            rows = tp[pl.ds((8 * j + 2 * z) * KB, 4 * KB), :]
            term = jnp.dot(jnp.concatenate(masked, axis=1), rows, preferred_element_type=jnp.float32)
            acc = term if acc is None else acc + term
    tail[pl.ds(0, ROWS), pl.ds(0, LEFT)] = acc[:, TILES * KB:]
    for a in range(A_ROW):
        for t in range(TILES):
            packed[a, pl.ds(8 + t * B_DEV, B_DEV), :] = acc[a * B_DEV:(a + 1) * B_DEV, t * KB:(t + 1) * KB]
        left = tail[pl.ds(a * B_DEV, 8, stride=8), :]
        for s in range(1, 8):
            left = left + pltpu.roll(tail[pl.ds(a * B_DEV + s, 8, stride=8), :], LEFT * s, 1)
        packed[a, pl.ds(0, 8), :] = left
    for z in range(4):
        mine_ref[z] = packed[2 * z + place[4]].astype(jnp.bfloat16)
        other_ref[z] = packed[2 * z + 1 - place[4]].astype(jnp.bfloat16)


def contract(table, w, t0, t1):
    ranks = w.shape[2]
    t_spec = pl.BlockSpec((4, D_DEV, 2 * N_DEV), lambda i, tab: (0, 0, 0))
    o_spec = pl.BlockSpec((4, PACKED, KB), lambda i, tab: (i, 0, 0))
    o_shape = jax.ShapeDtypeStruct((4 * GROUPS, PACKED, KB), jnp.bfloat16)
    return pl.pallas_call(
        contract_kernel,
        grid_spec=pltpu.PrefetchScalarGridSpec(
            num_scalar_prefetch=1,
            grid=(GROUPS,),
            in_specs=[
                pl.BlockSpec((1, 1, ranks, ROWS, KB), lambda i, tab: (i >> 1, (i & 1) ^ tab[7], 0, 0, 0)),
                t_spec,
                t_spec,
            ],
            out_specs=[o_spec, o_spec],
            scratch_shapes=[
                pltpu.VMEM((CB * KB, N_DEV), jnp.bfloat16),
                pltpu.VMEM((4, ROWS, KB), jnp.int32),
                pltpu.VMEM((2, ROWS, KB), jnp.int32),
                pltpu.VMEM((ROWS + 16, KB), jnp.float32),
                pltpu.VMEM((A_ROW, PACKED, KB), jnp.float32),
            ],
        ),
        out_shape=[o_shape, o_shape],
        compiler_params=pltpu.CompilerParams(vmem_limit_bytes=50 * 2**20),
        cost_estimate=pl.CostEstimate(flops=2 * 3200 * 2048 * 400, bytes_accessed=10000000, transcendentals=0),
        name="contract",
    )(table, w, t0, t1)


def add_kernel(in_ref, out_ref, tail, rows):
    for g in range(GROUPS):
        total = in_ref[4 * g].astype(jnp.float32)
        for z in range(1, 4):
            total = total + in_ref[4 * g + z].astype(jnp.float32)
        for t in range(TILES):
            rows[:, pl.ds(g * N_DEV + t * KB, KB)] = total[8 + t * B_DEV:8 + (t + 1) * B_DEV]
        for s in range(8):
            part = total[0:8] if s == 0 else pltpu.roll(total[0:8], KB - LEFT * s, 1)
            tail[pl.ds(s, 8, stride=8), :] = part
        rows[:, pl.ds(g * N_DEV + TILES * KB, LEFT)] = tail[pl.ds(0, B_DEV), pl.ds(0, LEFT)]
    out_ref[0] = rows[...].astype(jnp.bfloat16)


def add_up(parts):
    vmem = pl.BlockSpec(memory_space=pltpu.VMEM)
    return pl.pallas_call(
        add_kernel,
        in_specs=[vmem],
        out_specs=vmem,
        out_shape=jax.ShapeDtypeStruct((1, B_DEV, GROUPS * N_DEV), jnp.bfloat16),
        scratch_shapes=[pltpu.VMEM((64, KB), jnp.float32), pltpu.VMEM((B_DEV, GROUPS * N_DEV), jnp.float32)],
        compiler_params=pltpu.CompilerParams(vmem_limit_bytes=20 * 2**20),
        name="add_up",
    )(parts)


def program(ranks, table, integrals, amplitudes):
    f32, bf16 = jnp.float32, jnp.bfloat16
    w = squeeze(ranks, table, integrals)
    beside = lax.ppermute(w, "yn", SWAP)
    t = lax.all_to_all(amplitudes.reshape(25, GROUPS, N_DEV).transpose(1, 0, 2), ("x", "yn"), 0, 0, tiled=True)
    t = t.reshape(4, 2, 25, N_DEV).transpose(0, 2, 1, 3).reshape(1, D_DEV, 2 * N_DEV)
    t, w, beside = lax.optimization_barrier((t, w, beside))
    w = lax.all_gather(jnp.stack([w, beside]), "x", axis=0)
    t = lax.all_gather(t, "zh", axis=0, tiled=True)
    mine, other = contract(table, w, t, lax.ppermute(t, "yt", SWAP))
    got = lax.ppermute(other, "core", SWAP)
    total = (mine.astype(f32) + got.astype(f32)).astype(bf16)
    return add_up(lax.all_to_all(total, ("x", "yn", "zl"), 0, 0, tiled=True))


def shards(integrals, amplitudes, a_offsets, vir_offsets, c_offsets):
    x, zh, zl, core = (lax.axis_index(name) for name in ("x", "zh", "zl", "core"))
    yn, yt = lax.axis_index("yn"), lax.axis_index("yt")
    place = [(zh * 4 + yt) * B_DEV, (zl * 2 + core) * D_DEV, x, yt, core, 2 * yn, zl, yn]
    table = jnp.concatenate([jnp.stack(place).astype(jnp.int32), a_offsets, vir_offsets, c_offsets])
    few, most = functools.partial(program, RANKS_FEW), functools.partial(program, RANKS_MOST)
    narrow = jnp.max(c_offsets[1:] - c_offsets[:-1]) <= RANKS_FEW
    return lax.cond(narrow, few, most, table, integrals, amplitudes)


def solution(mesh):
    fine = Mesh(mesh.devices.reshape(4, 4, 2, 2, 4, 2), ("x", "zh", "yn", "yt", "zl", "core"))
    b_and_c = ("zh", "yn", "yt")
    in_specs = (P(b_and_c, ("zl", "core"), "x"), P(b_and_c, ("zl", "core", "x"), None), P(), P(), P())
    out_specs = P(("x", "zl", "core"), b_and_c, None)
    return jax.shard_map(shards, mesh=fine, in_specs=in_specs, out_specs=out_specs, check_vma=False)
```

```python
import functools

import jax
import jax.numpy as jnp
from jax import lax
from jax.experimental import pallas as pl
from jax.experimental.pallas import tpu as pltpu
from jax.sharding import Mesh, PartitionSpec as P

CB = 16
A_ROW = 8
B_DEV = 50
D_DEV = 100
N_DEV = 400
GROUPS = 8
ROWS = A_ROW * B_DEV
KB = 128
TILES = N_DEV // KB
LEFT = N_DEV - TILES * KB
PACKED = 160
SWAP = [(0, 1), (1, 0)]
RANKS_MOST = 9
RANKS_FEW = 3


def count_at_or_above(index, offsets):
    total = jnp.zeros_like(index)
    for k in range(1, 8):
        total = total + jnp.where(index >= offsets[k], 1, 0)
    return total


class Part:
    def __init__(self, table, start):
        self.table, self.start = table, start

    def __getitem__(self, k):
        return self.table[self.start + k]


def parts_of(table):
    return Part(table, 0), Part(table, 8), Part(table, 17), Part(table, 26)


def a_of(row):
    a = jnp.zeros_like(row)
    for k in range(1, A_ROW):
        a = a + jnp.where(row >= k * B_DEV, 1, 0)
    return a


def squeeze_kernel(ranks, table, v_ref, w_ref, by_b):
    place, a_off, v_off, c_off = parts_of(table)
    step = pl.program_id(0)
    b_step = v_ref.shape[0]
    lane = lax.broadcasted_iota(jnp.int32, (D_DEV, KB), 1)
    drow = lax.broadcasted_iota(jnp.int32, (D_DEV, KB), 0)
    base = count_at_or_above(drow + place[1], v_off)
    base = base ^ count_at_or_above((lane >> 4) + place[2] * A_ROW, a_off)
    base = base ^ count_at_or_above(lane & 15, c_off)
    elane = lax.broadcasted_iota(jnp.int32, (ranks * A_ROW, KB), 1)
    erow = lax.broadcasted_iota(jnp.int32, (ranks * A_ROW, KB), 0)
    c = elane & 15
    c_label = count_at_or_above(c, c_off)
    first = jnp.zeros_like(c)
    for k in range(8):
        first = first + jnp.where(c_label == k, c_off[k], 0)
    pick = ((elane >> 4) == (erow & 7)) & ((c - first) == (erow >> 3))
    pick = jnp.where(pick, 1.0, 0.0).astype(jnp.bfloat16)

    @pl.when(step == 0)
    def _():
        by_b[...] = jnp.zeros_like(by_b)

    b0 = place[0] + place[5] * B_DEV + step * b_step
    for p in range(b_step // 2):
        halves = []
        for q in range(2):
            b = 2 * p + q
            b_label = count_at_or_above(b0 + b, v_off)
            x = jnp.where(base == b_label, v_ref[b].astype(jnp.float32), 0.0).astype(jnp.bfloat16)
            halves.append(lax.dot_general(pick, x, (((1,), (1,)), ((), ())), preferred_element_type=jnp.float32))
        for r in range(ranks):
            pair = jnp.concatenate([h[r * A_ROW:(r + 1) * A_ROW] for h in halves], axis=0)
            start = pl.multiple_of(step * (b_step * A_ROW) + 16 * p, 16)
            by_b[r, pl.ds(start, 16), pl.ds(0, D_DEV)] = pair.astype(jnp.bfloat16)

    @pl.when(step == pl.num_programs(0) - 1)
    def _():
        to = lax.broadcasted_iota(jnp.int32, (ROWS, ROWS), 0)
        source = lax.broadcasted_iota(jnp.int32, (ROWS, ROWS), 1)
        a = a_of(to)
        move = jnp.where(source == (to - a * B_DEV) * A_ROW + a, 1.0, 0.0).astype(jnp.bfloat16)
        for r in range(ranks):
            w_ref[r] = jnp.dot(move, by_b[r], preferred_element_type=jnp.float32).astype(jnp.bfloat16)


SMEM = pl.BlockSpec(memory_space=pltpu.SMEM)


def squeeze(ranks, table, v):
    b_step = 10
    return pl.pallas_call(
        functools.partial(squeeze_kernel, ranks),
        grid=(B_DEV // b_step,),
        in_specs=[SMEM, pl.BlockSpec((b_step, D_DEV, KB), lambda i: (i, 0, 0))],
        out_specs=pl.BlockSpec((ranks, ROWS, KB), lambda i: (0, 0, 0)),
        out_shape=jax.ShapeDtypeStruct((ranks, ROWS, KB), jnp.bfloat16),
        scratch_shapes=[pltpu.VMEM((ranks, ROWS, KB), jnp.bfloat16)],
        compiler_params=pltpu.CompilerParams(vmem_limit_bytes=40 * 2**20),
        cost_estimate=pl.CostEstimate(flops=2 * 5000 * 128 * 8 * ranks, bytes_accessed=2400000, transcendentals=0),
        name="squeeze",
    )(table, v)


def fill_rows(tp, t):
    tp[...] = jnp.zeros_like(tp)
    for z in range(4):
        block = t[z].astype(jnp.float32)
        for h in range(2):
            part = block[:, h * N_DEV:(h + 1) * N_DEV].astype(jnp.bfloat16)
            tp[pl.ds((2 * z + h) * KB, D_DEV), :] = part


def fill_labels(table, a_labels, bd_labels):
    place, a_off, v_off, _ = parts_of(table)
    row = lax.broadcasted_iota(jnp.int32, (ROWS, KB), 0)
    lane = lax.broadcasted_iota(jnp.int32, (ROWS, KB), 1)
    a = a_of(row)
    d_label = count_at_or_above(lane + place[1], v_off)
    for s in range(4):
        a_labels[s] = count_at_or_above(a + s * A_ROW, a_off)
    for s in range(2):
        bd_labels[s] = d_label ^ count_at_or_above(row - a * B_DEV + place[0] + s * 2 * B_DEV, v_off)


def x_at(step, table):
    return (table[2] + (step >> 1)) & 3


def yn_at(step, table):
    return table[7] ^ (step & 1)


def product(table, step, w_ref, yt, tp, a_labels, bd_labels):
    c_off = parts_of(table)[3]
    base = (a_labels[x_at(step, table)] ^ bd_labels[yn_at(step, table)]).astype(jnp.float32).astype(jnp.bfloat16)
    masked = []
    for z in range(4):
        for h in range(2):
            c = 4 * z + 2 * h + yt
            c_label = count_at_or_above(c, c_off)
            rank = jnp.minimum(c - c_off[c_label], w_ref.shape[1] - 1)
            w = w_ref[step & 1, rank]
            hit = base == c_label.astype(jnp.float32).astype(jnp.bfloat16)
            masked.append(jnp.where(hit, w, jnp.zeros_like(w)))
    return jnp.dot(jnp.concatenate(masked, axis=1), tp[...], preferred_element_type=jnp.float32)


def early_kernel(table, w0, w1, w2, w3, t, out_ref, tp, a_labels, bd_labels):
    step = pl.program_id(0)

    @pl.when(step == 0)
    def _():
        fill_rows(tp, t)
        fill_labels(table, a_labels, bd_labels)

    for j, w in enumerate((w0, w1, w2, w3)):
        @pl.when(step >> 1 == j)
        def _(w=w):
            out_ref[0] = product(table, step, w, table[3], tp, a_labels, bd_labels)


def late_kernel(table, w0, w1, w2, w3, t, part_ref, mine_ref, other_ref, tp, a_labels, bd_labels, acc, tail, packed):
    step = pl.program_id(0)

    @pl.when(step == 0)
    def _():
        fill_rows(tp, t)
        fill_labels(table, a_labels, bd_labels)
        tail[...] = jnp.zeros_like(tail)
        packed[...] = jnp.zeros_like(packed)

    for j, w in enumerate((w0, w1, w2, w3)):
        @pl.when(step >> 1 == j)
        def _(w=w):
            acc[...] = part_ref[0] + product(table, step, w, 1 - table[3], tp, a_labels, bd_labels)

    tail[pl.ds(0, ROWS), pl.ds(0, LEFT)] = acc[:, TILES * KB:]
    for a in range(A_ROW):
        for s in range(TILES):
            packed[a, pl.ds(8 + s * B_DEV, B_DEV), :] = acc[a * B_DEV:(a + 1) * B_DEV, s * KB:(s + 1) * KB]
        left = tail[pl.ds(a * B_DEV, 8, stride=8), :]
        for s in range(1, 8):
            left = left + pltpu.roll(tail[pl.ds(a * B_DEV + s, 8, stride=8), :], LEFT * s, 1)
        packed[a, pl.ds(0, 8), :] = left
    for z in range(4):
        mine_ref[z] = packed[2 * z + table[4]].astype(jnp.bfloat16)
        other_ref[z] = packed[2 * z + 1 - table[4]].astype(jnp.bfloat16)


SCRATCH = [
    pltpu.VMEM((CB // 2 * KB, N_DEV), jnp.bfloat16),
    pltpu.VMEM((4, ROWS, KB), jnp.int32),
    pltpu.VMEM((2, ROWS, KB), jnp.int32),
]
PART = pl.BlockSpec((1, ROWS, N_DEV), lambda i, tab: (i, 0, 0))


def operands(ranks):
    w_spec = pl.BlockSpec((2, ranks, ROWS, KB), lambda i, tab: (0, 0, 0, 0))
    return [w_spec] * 4 + [pl.BlockSpec((4, D_DEV, 2 * N_DEV), lambda i, tab: (0, 0, 0))]


def early(table, ws, t):
    return pl.pallas_call(
        early_kernel,
        grid_spec=pltpu.PrefetchScalarGridSpec(
            num_scalar_prefetch=1,
            grid=(GROUPS,),
            in_specs=operands(ws[0].shape[1]),
            out_specs=PART,
            scratch_shapes=SCRATCH,
        ),
        out_shape=jax.ShapeDtypeStruct((GROUPS, ROWS, N_DEV), jnp.float32),
        compiler_params=pltpu.CompilerParams(vmem_limit_bytes=50 * 2**20),
        cost_estimate=pl.CostEstimate(flops=2 * 3200 * 1024 * 400, bytes_accessed=9000000, transcendentals=0),
        name="early",
    )(table, *ws, t)


def late(table, ws, t, partial):
    o_spec = pl.BlockSpec((4, PACKED, KB), lambda i, tab: (2 * x_at(i, tab) + yn_at(i, tab), 0, 0))
    o_shape = jax.ShapeDtypeStruct((4 * GROUPS, PACKED, KB), jnp.bfloat16)
    return pl.pallas_call(
        late_kernel,
        grid_spec=pltpu.PrefetchScalarGridSpec(
            num_scalar_prefetch=1,
            grid=(GROUPS,),
            in_specs=operands(ws[0].shape[1]) + [PART],
            out_specs=[o_spec, o_spec],
            scratch_shapes=SCRATCH + [
                pltpu.VMEM((ROWS, N_DEV), jnp.float32),
                pltpu.VMEM((ROWS + 16, KB), jnp.float32),
                pltpu.VMEM((A_ROW, PACKED, KB), jnp.float32),
            ],
        ),
        out_shape=[o_shape, o_shape],
        compiler_params=pltpu.CompilerParams(vmem_limit_bytes=50 * 2**20),
        cost_estimate=pl.CostEstimate(flops=2 * 3200 * 1024 * 400, bytes_accessed=11000000, transcendentals=0),
        name="late",
    )(table, *ws, t, partial)


def add_kernel(in_ref, out_ref, tail, rows):
    for g in range(GROUPS):
        total = in_ref[4 * g].astype(jnp.float32)
        for z in range(1, 4):
            total = total + in_ref[4 * g + z].astype(jnp.float32)
        for t in range(TILES):
            rows[:, pl.ds(g * N_DEV + t * KB, KB)] = total[8 + t * B_DEV:8 + (t + 1) * B_DEV]
        for s in range(8):
            part = total[0:8] if s == 0 else pltpu.roll(total[0:8], KB - LEFT * s, 1)
            tail[pl.ds(s, 8, stride=8), :] = part
        rows[:, pl.ds(g * N_DEV + TILES * KB, LEFT)] = tail[pl.ds(0, B_DEV), pl.ds(0, LEFT)]
    out_ref[0] = rows[...].astype(jnp.bfloat16)


def add_up(parts):
    vmem = pl.BlockSpec(memory_space=pltpu.VMEM)
    return pl.pallas_call(
        add_kernel,
        in_specs=[vmem],
        out_specs=vmem,
        out_shape=jax.ShapeDtypeStruct((1, B_DEV, GROUPS * N_DEV), jnp.bfloat16),
        scratch_shapes=[pltpu.VMEM((64, KB), jnp.float32), pltpu.VMEM((B_DEV, GROUPS * N_DEV), jnp.float32)],
        compiler_params=pltpu.CompilerParams(vmem_limit_bytes=20 * 2**20),
        name="add_up",
    )(parts)


def turn(k):
    return [(i, (i - k) % 4) for i in range(4)]


def around(w):
    return [w] + [lax.ppermute(w, "x", turn(k)) for k in (1, 2, 3)]


def again(table, integrals, ws, own, beside, partial):
    w = squeeze(RANKS_MOST, table, integrals)
    ws = around(jnp.stack([w, lax.ppermute(w, "yn", SWAP)]))
    return late(table, ws, beside, early(table, ws, own))


def finish(table, integrals, ws, own, beside, partial):
    return late(table, ws, beside, partial)


def shards(integrals, amplitudes, a_offsets, vir_offsets, c_offsets):
    f32, bf16 = jnp.float32, jnp.bfloat16
    x, zh, zl, core = (lax.axis_index(name) for name in ("x", "zh", "zl", "core"))
    yn, yt = lax.axis_index("yn"), lax.axis_index("yt")
    place = [(zh * 4 + yt) * B_DEV, (zl * 2 + core) * D_DEV, x, yt, core, 2 * yn, zl, yn]
    table = jnp.concatenate([jnp.stack(place).astype(jnp.int32), a_offsets, vir_offsets, c_offsets])
    narrow = jnp.max(c_offsets[1:] - c_offsets[:-1]) <= RANKS_FEW
    w = squeeze(RANKS_FEW, table, integrals)
    w_beside = lax.ppermute(w, "yn", SWAP)
    t = lax.all_to_all(amplitudes.reshape(25, GROUPS, N_DEV).transpose(1, 0, 2), ("x", "yn"), 0, 0, tiled=True)
    t = t.reshape(4, 2, 25, N_DEV).transpose(0, 2, 1, 3).reshape(1, D_DEV, 2 * N_DEV)
    t, w, w_beside = lax.optimization_barrier((t, w, w_beside))
    ws = around(jnp.stack([w, w_beside]))
    own = lax.all_gather(t, "zh", axis=0, tiled=True)
    beside = lax.ppermute(own, "yt", SWAP)
    partial = early(table, ws, own)
    mine, other = lax.cond(narrow, finish, again, table, integrals, ws, own, beside, partial)
    got = lax.ppermute(other, "core", SWAP)
    total = (mine.astype(f32) + got.astype(f32)).astype(bf16)
    return add_up(lax.all_to_all(total, ("x", "yn", "zl"), 0, 0, tiled=True))


def solution(mesh):
    fine = Mesh(mesh.devices.reshape(4, 4, 2, 2, 4, 2), ("x", "zh", "yn", "yt", "zl", "core"))
    b_and_c = ("zh", "yn", "yt")
    in_specs = (P(b_and_c, ("zl", "core"), "x"), P(b_and_c, ("zl", "core", "x"), None), P(), P(), P())
    out_specs = P(("x", "zl", "core"), b_and_c, None)
    return jax.shard_map(shards, mesh=fine, in_specs=in_specs, out_specs=out_specs, check_vma=False)
```

```python
import functools

import jax
import jax.numpy as jnp
from jax import lax
from jax.experimental import pallas as pl
from jax.experimental.pallas import tpu as pltpu
from jax.sharding import Mesh, PartitionSpec as P

CB = 16
A_ROW = 8
B_DEV = 50
D_DEV = 100
D_ROW = 25
CHUNK = 80
N_DEV = 400
GROUPS = 8
ROWS = A_ROW * B_DEV
KB = 128
TILES = N_DEV // KB
LEFT = N_DEV - TILES * KB
PACKED = 160
SWAP = [(0, 1), (1, 0)]
RANKS_MOST = 9
RANKS_FEW = 3


def count_at_or_above(index, offsets):
    total = jnp.zeros_like(index)
    for k in range(1, 8):
        total = total + jnp.where(index >= offsets[k], 1, 0)
    return total


class Part:
    def __init__(self, table, start):
        self.table, self.start = table, start

    def __getitem__(self, k):
        return self.table[self.start + k]


def parts_of(table):
    return Part(table, 0), Part(table, 8), Part(table, 17), Part(table, 26)


def a_of(row):
    a = jnp.zeros_like(row)
    for k in range(1, A_ROW):
        a = a + jnp.where(row >= k * B_DEV, 1, 0)
    return a


def squeeze_kernel(ranks, table, v_ref, w_ref, by_b):
    place, a_off, v_off, c_off = parts_of(table)
    step = pl.program_id(0)
    b_step = v_ref.shape[0]
    lane = lax.broadcasted_iota(jnp.int32, (D_DEV, KB), 1)
    drow = lax.broadcasted_iota(jnp.int32, (D_DEV, KB), 0)
    base = count_at_or_above(drow + place[1], v_off)
    base = base ^ count_at_or_above((lane >> 4) + place[2] * A_ROW, a_off)
    base = base ^ count_at_or_above(lane & 15, c_off)
    elane = lax.broadcasted_iota(jnp.int32, (ranks * A_ROW, KB), 1)
    erow = lax.broadcasted_iota(jnp.int32, (ranks * A_ROW, KB), 0)
    c = elane & 15
    c_label = count_at_or_above(c, c_off)
    first = jnp.zeros_like(c)
    for k in range(8):
        first = first + jnp.where(c_label == k, c_off[k], 0)
    pick = ((elane >> 4) == (erow & 7)) & ((c - first) == (erow >> 3))
    pick = jnp.where(pick, 1.0, 0.0).astype(jnp.bfloat16)

    @pl.when(step == 0)
    def _():
        by_b[...] = jnp.zeros_like(by_b)

    b0 = place[0] + place[5] * B_DEV + step * b_step
    for p in range(b_step // 2):
        halves = []
        for q in range(2):
            b = 2 * p + q
            b_label = count_at_or_above(b0 + b, v_off)
            x = jnp.where(base == b_label, v_ref[b].astype(jnp.float32), 0.0).astype(jnp.bfloat16)
            halves.append(lax.dot_general(pick, x, (((1,), (1,)), ((), ())), preferred_element_type=jnp.float32))
        for r in range(ranks):
            pair = jnp.concatenate([h[r * A_ROW:(r + 1) * A_ROW] for h in halves], axis=0)
            start = pl.multiple_of(step * (b_step * A_ROW) + 16 * p, 16)
            by_b[r, pl.ds(start, 16), pl.ds(0, D_DEV)] = pair.astype(jnp.bfloat16)

    @pl.when(step == pl.num_programs(0) - 1)
    def _():
        to = lax.broadcasted_iota(jnp.int32, (ROWS, ROWS), 0)
        source = lax.broadcasted_iota(jnp.int32, (ROWS, ROWS), 1)
        a = a_of(to)
        move = jnp.where(source == (to - a * B_DEV) * A_ROW + a, 1.0, 0.0).astype(jnp.bfloat16)
        for r in range(ranks):
            w_ref[r] = jnp.dot(move, by_b[r], preferred_element_type=jnp.float32).astype(jnp.bfloat16)


SMEM = pl.BlockSpec(memory_space=pltpu.SMEM)


def squeeze(ranks, table, v):
    b_step = 10
    return pl.pallas_call(
        functools.partial(squeeze_kernel, ranks),
        grid=(B_DEV // b_step,),
        in_specs=[SMEM, pl.BlockSpec((b_step, D_DEV, KB), lambda i: (i, 0, 0))],
        out_specs=pl.BlockSpec((ranks, ROWS, KB), lambda i: (0, 0, 0)),
        out_shape=jax.ShapeDtypeStruct((ranks, ROWS, KB), jnp.bfloat16),
        scratch_shapes=[pltpu.VMEM((ranks, ROWS, KB), jnp.bfloat16)],
        compiler_params=pltpu.CompilerParams(vmem_limit_bytes=40 * 2**20),
        cost_estimate=pl.CostEstimate(flops=2 * 5000 * 128 * 8 * ranks, bytes_accessed=2400000, transcendentals=0),
        name="squeeze",
    )(table, v)


def pack_kernel(t_ref, out_ref, rows, tail):
    rows[...] = jnp.zeros_like(rows)
    tail[...] = jnp.zeros_like(tail)
    for g in range(GROUPS):
        block = t_ref[0, :, g * N_DEV:(g + 1) * N_DEV].astype(jnp.float32)
        for s in range(TILES):
            rows[pl.ds(g * CHUNK + s * D_ROW, D_ROW), :] = block[:, s * KB:(s + 1) * KB]
        tail[pl.ds(0, D_ROW), pl.ds(0, LEFT)] = block[:, TILES * KB:]
        left = tail[pl.ds(0, 4, stride=8), :]
        for s in range(1, 8):
            left = left + pltpu.roll(tail[pl.ds(s, 4, stride=8), :], LEFT * s, 1)
        rows[pl.ds(g * CHUNK + TILES * D_ROW, 4), :] = left
    out_ref[...] = rows[...].astype(jnp.bfloat16)


def pack(t):
    vmem = pl.BlockSpec(memory_space=pltpu.VMEM)
    return pl.pallas_call(
        pack_kernel,
        in_specs=[vmem],
        out_specs=vmem,
        out_shape=jax.ShapeDtypeStruct((GROUPS * CHUNK, KB), jnp.bfloat16),
        scratch_shapes=[pltpu.VMEM((GROUPS * CHUNK, KB), jnp.float32), pltpu.VMEM((32, KB), jnp.float32)],
        compiler_params=pltpu.CompilerParams(vmem_limit_bytes=8 * 2**20),
        name="pack",
    )(t)


def fill_rows(tp, t, block, tail):
    block[...] = jnp.zeros_like(block)

    @pl.loop(0, CB // 2)
    def _(i):
        for x in range(4):
            start = pl.multiple_of(((i >> 1) * GROUPS + 2 * x + (i & 1)) * CHUNK, 16)
            chunk = t[pl.ds(start, CHUNK), :].astype(jnp.float32)
            for s in range(TILES):
                block[pl.ds(x * D_ROW, D_ROW), pl.ds(s * KB, KB)] = chunk[s * D_ROW:(s + 1) * D_ROW]
            left = chunk[TILES * D_ROW:TILES * D_ROW + 4]
            for s in range(8):
                tail[x, pl.ds(s, 4, stride=8), :] = left if s == 0 else pltpu.roll(left, KB - LEFT * s, 1)
            block[pl.ds(x * D_ROW, D_ROW), pl.ds(TILES * KB, LEFT)] = tail[x, pl.ds(0, D_ROW), pl.ds(0, LEFT)]
        tp[pl.ds(pl.multiple_of(i * KB, KB), KB), :] = block[...].astype(jnp.bfloat16)


def fill_labels(table, base, a_labels):
    place, a_off, v_off, _ = parts_of(table)
    row = lax.broadcasted_iota(jnp.int32, (ROWS, KB), 0)
    lane = lax.broadcasted_iota(jnp.int32, (ROWS, KB), 1)
    a = a_of(row)
    d_label = count_at_or_above(lane + place[1], v_off)
    for s in range(4):
        a_labels[s] = count_at_or_above(a + s * A_ROW, a_off)
    for h in range(2):
        first = place[0] + yn_at(h, table) * 2 * B_DEV
        bd_label = d_label ^ count_at_or_above(row - a * B_DEV + first, v_off)

        @pl.loop(0, 4)
        def _(j):
            base[j, h] = (bd_label ^ a_labels[x_at(2 * j, table)]).astype(jnp.float32).astype(jnp.bfloat16)


def x_at(step, table):
    return (table[2] + (step >> 1)) & 3


def yn_at(step, table):
    return table[7] ^ (step & 1)


def product(table, j, w_ref, yt, tp, base):
    c_off = parts_of(table)[3]
    halves = []
    for h in range(2):
        labels = base[j, h]
        masked = []
        for i in range(CB // 2):
            c = 2 * i + yt
            c_label = count_at_or_above(c, c_off)
            rank = jnp.minimum(c - c_off[c_label], w_ref.shape[2] - 1)
            w = w_ref[j, h, rank]
            hit = labels == c_label.astype(jnp.float32).astype(jnp.bfloat16)
            masked.append(jnp.where(hit, w, jnp.zeros_like(w)))
        halves.append(jnp.concatenate(masked, axis=1))
    return jnp.dot(jnp.concatenate(halves, axis=0), tp[...], preferred_element_type=jnp.float32)


def early_kernel(table, w_ref, t, out_ref, base, tp, block, tail, a_labels):
    fill_rows(tp, t, block, tail)
    fill_labels(table, base, a_labels)

    @pl.loop(0, 4)
    def _(j):
        out_ref[j] = product(table, j, w_ref, table[3], tp, base)


def late_kernel(table, w_ref, t, part_ref, base, mine_ref, other_ref, tp, block, tail, acc, side, packed):
    fill_rows(tp, t, block, tail)
    side[...] = jnp.zeros_like(side)
    packed[...] = jnp.zeros_like(packed)

    @pl.loop(0, 4)
    def _(j):
        acc[...] = part_ref[j] + product(table, j, w_ref, 1 - table[3], tp, base)

        @pl.loop(0, 2)
        def _(h):
            part = acc.at[pl.ds(pl.multiple_of(h * ROWS, 8), ROWS)]
            side[pl.ds(0, ROWS), pl.ds(0, LEFT)] = part[:, TILES * KB:]
            for a in range(A_ROW):
                for s in range(TILES):
                    packed[a, pl.ds(8 + s * B_DEV, B_DEV), :] = part[a * B_DEV:(a + 1) * B_DEV, s * KB:(s + 1) * KB]
                left = side[pl.ds(a * B_DEV, 8, stride=8), :]
                for s in range(1, 8):
                    left = left + pltpu.roll(side[pl.ds(a * B_DEV + s, 8, stride=8), :], LEFT * s, 1)
                packed[a, pl.ds(0, 8), :] = left
            to = 4 * (2 * x_at(2 * j, table) + yn_at(h, table))
            for z in range(4):
                mine_ref[to + z] = packed[2 * z + table[4]].astype(jnp.bfloat16)
                other_ref[to + z] = packed[2 * z + 1 - table[4]].astype(jnp.bfloat16)


SCRATCH = [
    pltpu.VMEM((CB // 2 * KB, N_DEV), jnp.bfloat16),
    pltpu.VMEM((KB, N_DEV), jnp.float32),
    pltpu.VMEM((4, 32, KB), jnp.float32),
]
VMEM = pl.BlockSpec(memory_space=pltpu.VMEM)


def early(table, w, t):
    return pl.pallas_call(
        early_kernel,
        in_specs=[SMEM] + [VMEM] * 2,
        out_specs=[VMEM, VMEM],
        out_shape=[
            jax.ShapeDtypeStruct((4, 2 * ROWS, N_DEV), jnp.float32),
            jax.ShapeDtypeStruct((4, 2, ROWS, KB), jnp.bfloat16),
        ],
        scratch_shapes=SCRATCH + [pltpu.VMEM((4, ROWS, KB), jnp.int32)],
        compiler_params=pltpu.CompilerParams(vmem_limit_bytes=32 * 2**20),
        cost_estimate=pl.CostEstimate(flops=2 * 3200 * 1024 * 400, bytes_accessed=9000000, transcendentals=0),
        name="early",
    )(table, w, t)


def late(table, w, t, partial, base):
    o_shape = jax.ShapeDtypeStruct((4 * GROUPS, PACKED, KB), jnp.bfloat16)
    return pl.pallas_call(
        late_kernel,
        in_specs=[SMEM] + [VMEM] * 4,
        out_specs=[VMEM, VMEM],
        out_shape=[o_shape, o_shape],
        scratch_shapes=SCRATCH + [
            pltpu.VMEM((2 * ROWS, N_DEV), jnp.float32),
            pltpu.VMEM((ROWS + 16, KB), jnp.float32),
            pltpu.VMEM((A_ROW, PACKED, KB), jnp.float32),
        ],
        compiler_params=pltpu.CompilerParams(vmem_limit_bytes=32 * 2**20),
        cost_estimate=pl.CostEstimate(flops=2 * 3200 * 1024 * 400, bytes_accessed=11000000, transcendentals=0),
        name="late",
    )(table, w, t, partial, base)


def add_kernel(in_ref, out_ref, tail, rows):
    for g in range(GROUPS):
        total = in_ref[4 * g].astype(jnp.float32)
        for z in range(1, 4):
            total = total + in_ref[4 * g + z].astype(jnp.float32)
        for t in range(TILES):
            rows[:, pl.ds(g * N_DEV + t * KB, KB)] = total[8 + t * B_DEV:8 + (t + 1) * B_DEV]
        for s in range(8):
            part = total[0:8] if s == 0 else pltpu.roll(total[0:8], KB - LEFT * s, 1)
            tail[pl.ds(s, 8, stride=8), :] = part
        rows[:, pl.ds(g * N_DEV + TILES * KB, LEFT)] = tail[pl.ds(0, B_DEV), pl.ds(0, LEFT)]
    out_ref[0] = rows[...].astype(jnp.bfloat16)


def add_up(parts):
    vmem = pl.BlockSpec(memory_space=pltpu.VMEM)
    return pl.pallas_call(
        add_kernel,
        in_specs=[vmem],
        out_specs=vmem,
        out_shape=jax.ShapeDtypeStruct((1, B_DEV, GROUPS * N_DEV), jnp.bfloat16),
        scratch_shapes=[pltpu.VMEM((64, KB), jnp.float32), pltpu.VMEM((B_DEV, GROUPS * N_DEV), jnp.float32)],
        compiler_params=pltpu.CompilerParams(vmem_limit_bytes=20 * 2**20),
        name="add_up",
    )(parts)


def turn(k):
    return [(i, (i - k) % 4) for i in range(4)]


def around(w):
    return jnp.stack([w] + [lax.ppermute(w, "x", turn(k)) for k in (1, 2, 3)])


def again(table, integrals, w, own, beside, *done):
    w = squeeze(RANKS_MOST, table, integrals)
    w = around(jnp.stack([w, lax.ppermute(w, "yn", SWAP)]))
    return late(table, w, beside, *early(table, w, own))


def finish(table, integrals, w, own, beside, *done):
    return late(table, w, beside, *done)


def shards(integrals, amplitudes, a_offsets, vir_offsets, c_offsets):
    f32, bf16 = jnp.float32, jnp.bfloat16
    x, zh, zl, core = (lax.axis_index(name) for name in ("x", "zh", "zl", "core"))
    yn, yt = lax.axis_index("yn"), lax.axis_index("yt")
    place = [(zh * 4 + yt) * B_DEV, (zl * 2 + core) * D_DEV, x, yt, core, 2 * yn, zl, yn]
    table = jnp.concatenate([jnp.stack(place).astype(jnp.int32), a_offsets, vir_offsets, c_offsets])
    narrow = jnp.max(c_offsets[1:] - c_offsets[:-1]) <= RANKS_FEW
    w = squeeze(RANKS_FEW, table, integrals)
    w_beside = lax.ppermute(w, "yn", SWAP)
    t = lax.all_to_all(pack(amplitudes), ("x", "yn"), 0, 0, tiled=True)
    t, w, w_beside = lax.optimization_barrier((t, w, w_beside))
    w = around(jnp.stack([w, w_beside]))
    own = lax.all_gather(t, "zh", axis=0, tiled=True)
    beside = lax.ppermute(own, "yt", SWAP)
    mine, other = lax.cond(narrow, finish, again, table, integrals, w, own, beside, *early(table, w, own))
    got = lax.ppermute(other, "core", SWAP)
    total = (mine.astype(f32) + got.astype(f32)).astype(bf16)
    return add_up(lax.all_to_all(total, ("x", "yn", "zl"), 0, 0, tiled=True))


def solution(mesh):
    fine = Mesh(mesh.devices.reshape(4, 4, 2, 2, 4, 2), ("x", "zh", "yn", "yt", "zl", "core"))
    b_and_c = ("zh", "yn", "yt")
    in_specs = (P(b_and_c, ("zl", "core"), "x"), P(b_and_c, ("zl", "core", "x"), None), P(), P(), P())
    out_specs = P(("x", "zl", "core"), b_and_c, None)
    return jax.shard_map(shards, mesh=fine, in_specs=in_specs, out_specs=out_specs, check_vma=False)
```

```python
import functools

import jax
import jax.numpy as jnp
from jax import lax
from jax.experimental import pallas as pl
from jax.experimental.pallas import tpu as pltpu
from jax.sharding import Mesh, PartitionSpec as P

CB = 16
A_ROW = 8
B_DEV = 50
D_DEV = 100
D_ROW = 25
CHUNK = 80
N_DEV = 400
GROUPS = 8
ROWS = A_ROW * B_DEV
KB = 128
TILES = N_DEV // KB
LEFT = N_DEV - TILES * KB
PACKED = 160
SWAP = [(0, 1), (1, 0)]
RANKS_MOST = 9
RANKS_FEW = 3


def count_at_or_above(index, offsets):
    total = jnp.zeros_like(index)
    for k in range(1, 8):
        total = total + jnp.where(index >= offsets[k], 1, 0)
    return total


class Part:
    def __init__(self, table, start):
        self.table, self.start = table, start

    def __getitem__(self, k):
        return self.table[self.start + k]


def parts_of(table):
    return Part(table, 0), Part(table, 8), Part(table, 17), Part(table, 26)


def a_of(row):
    a = jnp.zeros_like(row)
    for k in range(1, A_ROW):
        a = a + jnp.where(row >= k * B_DEV, 1, 0)
    return a


def squeeze_kernel(ranks, table, v_ref, w_ref, by_b):
    place, a_off, v_off, c_off = parts_of(table)
    step = pl.program_id(0)
    b_step = v_ref.shape[0]
    lane = lax.broadcasted_iota(jnp.int32, (D_DEV, KB), 1)
    drow = lax.broadcasted_iota(jnp.int32, (D_DEV, KB), 0)
    base = count_at_or_above(drow + place[1], v_off)
    base = base ^ count_at_or_above((lane >> 4) + place[2] * A_ROW, a_off)
    base = base ^ count_at_or_above(lane & 15, c_off)
    elane = lax.broadcasted_iota(jnp.int32, (ranks * A_ROW, KB), 1)
    erow = lax.broadcasted_iota(jnp.int32, (ranks * A_ROW, KB), 0)
    c = elane & 15
    c_label = count_at_or_above(c, c_off)
    first = jnp.zeros_like(c)
    for k in range(8):
        first = first + jnp.where(c_label == k, c_off[k], 0)
    pick = ((elane >> 4) == (erow & 7)) & ((c - first) == (erow >> 3))
    pick = jnp.where(pick, 1.0, 0.0).astype(jnp.bfloat16)

    @pl.when(step == 0)
    def _():
        by_b[...] = jnp.zeros_like(by_b)

    b0 = place[0] + place[5] * B_DEV + step * b_step
    for p in range(b_step // 2):
        halves = []
        for q in range(2):
            b = 2 * p + q
            b_label = count_at_or_above(b0 + b, v_off)
            x = jnp.where(base == b_label, v_ref[b].astype(jnp.float32), 0.0).astype(jnp.bfloat16)
            halves.append(lax.dot_general(pick, x, (((1,), (1,)), ((), ())), preferred_element_type=jnp.float32))
        for r in range(ranks):
            pair = jnp.concatenate([h[r * A_ROW:(r + 1) * A_ROW] for h in halves], axis=0)
            start = pl.multiple_of(step * (b_step * A_ROW) + 16 * p, 16)
            by_b[r, pl.ds(start, 16), pl.ds(0, D_DEV)] = pair.astype(jnp.bfloat16)

    @pl.when(step == pl.num_programs(0) - 1)
    def _():
        to = lax.broadcasted_iota(jnp.int32, (ROWS, ROWS), 0)
        source = lax.broadcasted_iota(jnp.int32, (ROWS, ROWS), 1)
        a = a_of(to)
        move = jnp.where(source == (to - a * B_DEV) * A_ROW + a, 1.0, 0.0).astype(jnp.bfloat16)
        for r in range(ranks):
            w_ref[r] = jnp.dot(move, by_b[r], preferred_element_type=jnp.float32).astype(jnp.bfloat16)


SMEM = pl.BlockSpec(memory_space=pltpu.SMEM)


def squeeze(ranks, table, v):
    b_step = B_DEV
    return pl.pallas_call(
        functools.partial(squeeze_kernel, ranks),
        grid=(B_DEV // b_step,),
        in_specs=[SMEM, pl.BlockSpec((b_step, D_DEV, KB), lambda i: (i, 0, 0))],
        out_specs=pl.BlockSpec((ranks, ROWS, KB), lambda i: (0, 0, 0)),
        out_shape=jax.ShapeDtypeStruct((ranks, ROWS, KB), jnp.bfloat16),
        scratch_shapes=[pltpu.VMEM((ranks, ROWS, KB), jnp.bfloat16)],
        compiler_params=pltpu.CompilerParams(vmem_limit_bytes=40 * 2**20),
        cost_estimate=pl.CostEstimate(flops=2 * 5000 * 128 * 8 * ranks, bytes_accessed=2400000, transcendentals=0),
        name="squeeze",
    )(table, v)


def pack_kernel(t_ref, out_ref, rows, tail):
    rows[...] = jnp.zeros_like(rows)
    tail[...] = jnp.zeros_like(tail)
    for g in range(GROUPS):
        block = t_ref[0, :, g * N_DEV:(g + 1) * N_DEV].astype(jnp.float32)
        for s in range(TILES):
            rows[pl.ds(g * CHUNK + s * D_ROW, D_ROW), :] = block[:, s * KB:(s + 1) * KB]
        tail[pl.ds(0, D_ROW), pl.ds(0, LEFT)] = block[:, TILES * KB:]
        left = tail[pl.ds(0, 4, stride=8), :]
        for s in range(1, 8):
            left = left + pltpu.roll(tail[pl.ds(s, 4, stride=8), :], LEFT * s, 1)
        rows[pl.ds(g * CHUNK + TILES * D_ROW, 4), :] = left
    out_ref[...] = rows[...].astype(jnp.bfloat16)


def pack(t):
    vmem = pl.BlockSpec(memory_space=pltpu.VMEM)
    return pl.pallas_call(
        pack_kernel,
        in_specs=[vmem],
        out_specs=vmem,
        out_shape=jax.ShapeDtypeStruct((GROUPS * CHUNK, KB), jnp.bfloat16),
        scratch_shapes=[pltpu.VMEM((GROUPS * CHUNK, KB), jnp.float32), pltpu.VMEM((32, KB), jnp.float32)],
        compiler_params=pltpu.CompilerParams(vmem_limit_bytes=8 * 2**20),
        name="pack",
    )(t)


def fill_rows(tp, t, block, tail):
    block[...] = jnp.zeros_like(block)

    @pl.loop(0, CB // 2)
    def _(i):
        for x in range(4):
            start = pl.multiple_of(((i >> 1) * GROUPS + 2 * x + (i & 1)) * CHUNK, 16)
            chunk = t[pl.ds(start, CHUNK), :].astype(jnp.float32)
            for s in range(TILES):
                block[pl.ds(x * D_ROW, D_ROW), pl.ds(s * KB, KB)] = chunk[s * D_ROW:(s + 1) * D_ROW]
            left = chunk[TILES * D_ROW:TILES * D_ROW + 4]
            for s in range(8):
                tail[x, pl.ds(s, 4, stride=8), :] = left if s == 0 else pltpu.roll(left, KB - LEFT * s, 1)
            block[pl.ds(x * D_ROW, D_ROW), pl.ds(TILES * KB, LEFT)] = tail[x, pl.ds(0, D_ROW), pl.ds(0, LEFT)]
        tp[pl.ds(pl.multiple_of(i * KB, KB), KB), :] = block[...].astype(jnp.bfloat16)


def fill_labels(table, base, a_labels):
    place, a_off, v_off, _ = parts_of(table)
    row = lax.broadcasted_iota(jnp.int32, (ROWS, KB), 0)
    lane = lax.broadcasted_iota(jnp.int32, (ROWS, KB), 1)
    a = a_of(row)
    d_label = count_at_or_above(lane + place[1], v_off)
    for s in range(4):
        a_labels[s] = count_at_or_above(a + s * A_ROW, a_off)
    for h in range(2):
        first = place[0] + yn_at(h, table) * 2 * B_DEV
        bd_label = d_label ^ count_at_or_above(row - a * B_DEV + first, v_off)

        @pl.loop(0, 4)
        def _(j):
            base[j, h] = (bd_label ^ a_labels[x_at(2 * j, table)]).astype(jnp.float32).astype(jnp.bfloat16)


def x_at(step, table):
    return (table[2] + (step >> 1)) & 3


def yn_at(step, table):
    return table[7] ^ (step & 1)


def product(table, j, w_ref, yt, tp, base):
    c_off = parts_of(table)[3]
    halves = []
    for h in range(2):
        labels = base[j, h]
        masked = []
        for i in range(CB // 2):
            c = 2 * i + yt
            c_label = count_at_or_above(c, c_off)
            rank = jnp.minimum(c - c_off[c_label], w_ref.shape[2] - 1)
            w = w_ref[j, h, rank]
            hit = labels == c_label.astype(jnp.float32).astype(jnp.bfloat16)
            masked.append(jnp.where(hit, w, jnp.zeros_like(w)))
        halves.append(jnp.concatenate(masked, axis=1))
    return jnp.dot(jnp.concatenate(halves, axis=0), tp[...], preferred_element_type=jnp.float32)


def early_kernel(table, w_ref, t, out_ref, base, tp, block, tail, a_labels):
    fill_rows(tp, t, block, tail)
    fill_labels(table, base, a_labels)

    @pl.loop(0, 4)
    def _(j):
        out_ref[j] = product(table, j, w_ref, table[3], tp, base)


def late_kernel(table, w_ref, t, part_ref, base, mine_ref, other_ref, tp, block, tail, acc, side, packed):
    fill_rows(tp, t, block, tail)
    side[...] = jnp.zeros_like(side)
    packed[...] = jnp.zeros_like(packed)

    @pl.loop(0, 4)
    def _(j):
        acc[...] = part_ref[j] + product(table, j, w_ref, 1 - table[3], tp, base)

        @pl.loop(0, 2)
        def _(h):
            part = acc.at[pl.ds(pl.multiple_of(h * ROWS, 8), ROWS)]
            side[pl.ds(0, ROWS), pl.ds(0, LEFT)] = part[:, TILES * KB:]
            for a in range(A_ROW):
                for s in range(TILES):
                    packed[a, pl.ds(8 + s * B_DEV, B_DEV), :] = part[a * B_DEV:(a + 1) * B_DEV, s * KB:(s + 1) * KB]
                left = side[pl.ds(a * B_DEV, 8, stride=8), :]
                for s in range(1, 8):
                    left = left + pltpu.roll(side[pl.ds(a * B_DEV + s, 8, stride=8), :], LEFT * s, 1)
                packed[a, pl.ds(0, 8), :] = left
            to = 4 * (2 * x_at(2 * j, table) + yn_at(h, table))
            for z in range(4):
                mine_ref[to + z] = packed[2 * z + table[4]].astype(jnp.bfloat16)
                other_ref[to + z] = packed[2 * z + 1 - table[4]].astype(jnp.bfloat16)


SCRATCH = [
    pltpu.VMEM((CB // 2 * KB, N_DEV), jnp.bfloat16),
    pltpu.VMEM((KB, N_DEV), jnp.float32),
    pltpu.VMEM((4, 32, KB), jnp.float32),
]
VMEM = pl.BlockSpec(memory_space=pltpu.VMEM)


def early(table, w, t):
    return pl.pallas_call(
        early_kernel,
        in_specs=[SMEM] + [VMEM] * 2,
        out_specs=[VMEM, VMEM],
        out_shape=[
            jax.ShapeDtypeStruct((4, 2 * ROWS, N_DEV), jnp.float32),
            jax.ShapeDtypeStruct((4, 2, ROWS, KB), jnp.bfloat16),
        ],
        scratch_shapes=SCRATCH + [pltpu.VMEM((4, ROWS, KB), jnp.int32)],
        compiler_params=pltpu.CompilerParams(vmem_limit_bytes=32 * 2**20),
        cost_estimate=pl.CostEstimate(flops=2 * 3200 * 1024 * 400, bytes_accessed=9000000, transcendentals=0),
        name="early",
    )(table, w, t)


def late(table, w, t, partial, base):
    o_shape = jax.ShapeDtypeStruct((4 * GROUPS, PACKED, KB), jnp.bfloat16)
    return pl.pallas_call(
        late_kernel,
        in_specs=[SMEM] + [VMEM] * 4,
        out_specs=[VMEM, VMEM],
        out_shape=[o_shape, o_shape],
        scratch_shapes=SCRATCH + [
            pltpu.VMEM((2 * ROWS, N_DEV), jnp.float32),
            pltpu.VMEM((ROWS + 16, KB), jnp.float32),
            pltpu.VMEM((A_ROW, PACKED, KB), jnp.float32),
        ],
        compiler_params=pltpu.CompilerParams(vmem_limit_bytes=32 * 2**20),
        cost_estimate=pl.CostEstimate(flops=2 * 3200 * 1024 * 400, bytes_accessed=11000000, transcendentals=0),
        name="late",
    )(table, w, t, partial, base)


def add_kernel(in_ref, out_ref, tail, rows):
    for g in range(GROUPS):
        total = in_ref[4 * g].astype(jnp.float32)
        for z in range(1, 4):
            total = total + in_ref[4 * g + z].astype(jnp.float32)
        for t in range(TILES):
            rows[:, pl.ds(g * N_DEV + t * KB, KB)] = total[8 + t * B_DEV:8 + (t + 1) * B_DEV]
        for s in range(8):
            part = total[0:8] if s == 0 else pltpu.roll(total[0:8], KB - LEFT * s, 1)
            tail[pl.ds(s, 8, stride=8), :] = part
        rows[:, pl.ds(g * N_DEV + TILES * KB, LEFT)] = tail[pl.ds(0, B_DEV), pl.ds(0, LEFT)]
    out_ref[0] = rows[...].astype(jnp.bfloat16)


def add_up(parts):
    vmem = pl.BlockSpec(memory_space=pltpu.VMEM)
    return pl.pallas_call(
        add_kernel,
        in_specs=[vmem],
        out_specs=vmem,
        out_shape=jax.ShapeDtypeStruct((1, B_DEV, GROUPS * N_DEV), jnp.bfloat16),
        scratch_shapes=[pltpu.VMEM((64, KB), jnp.float32), pltpu.VMEM((B_DEV, GROUPS * N_DEV), jnp.float32)],
        compiler_params=pltpu.CompilerParams(vmem_limit_bytes=20 * 2**20),
        name="add_up",
    )(parts)


def turn(k):
    return [(i, (i - k) % 4) for i in range(4)]


def around(w):
    return jnp.stack([w] + [lax.ppermute(w, "x", turn(k)) for k in (1, 2, 3)])


def again(table, integrals, w, own, beside, *done):
    w = squeeze(RANKS_MOST, table, integrals)
    w = around(jnp.stack([w, lax.ppermute(w, "yn", SWAP)]))
    return late(table, w, beside, *early(table, w, own))


def finish(table, integrals, w, own, beside, *done):
    return late(table, w, beside, *done)


def shards(integrals, amplitudes, a_offsets, vir_offsets, c_offsets):
    f32, bf16 = jnp.float32, jnp.bfloat16
    x, zh, zl, core = (lax.axis_index(name) for name in ("x", "zh", "zl", "core"))
    yn, yt = lax.axis_index("yn"), lax.axis_index("yt")
    place = [(zh * 4 + yt) * B_DEV, (zl * 2 + core) * D_DEV, x, yt, core, 2 * yn, zl, yn]
    table = jnp.concatenate([jnp.stack(place).astype(jnp.int32), a_offsets, vir_offsets, c_offsets])
    narrow = jnp.max(c_offsets[1:] - c_offsets[:-1]) <= RANKS_FEW
    w = squeeze(RANKS_FEW, table, integrals)
    w_beside = lax.ppermute(w, "yn", SWAP)
    t = lax.all_to_all(pack(amplitudes), ("x", "yn"), 0, 0, tiled=True)
    t, w, w_beside = lax.optimization_barrier((t, w, w_beside))
    w = around(jnp.stack([w, w_beside]))
    own = lax.all_gather(t, "zh", axis=0, tiled=True)
    beside = lax.ppermute(own, "yt", SWAP)
    mine, other = lax.cond(narrow, finish, again, table, integrals, w, own, beside, *early(table, w, own))
    got = lax.ppermute(other, "core", SWAP)
    total = (mine.astype(f32) + got.astype(f32)).astype(bf16)
    return add_up(lax.all_to_all(total, ("x", "yn", "zl"), 0, 0, tiled=True))


def solution(mesh):
    fine = Mesh(mesh.devices.reshape(4, 4, 2, 2, 4, 2), ("x", "zh", "yn", "yt", "zl", "core"))
    b_and_c = ("zh", "yn", "yt")
    in_specs = (P(b_and_c, ("zl", "core"), "x"), P(b_and_c, ("zl", "core", "x"), None), P(), P(), P())
    out_specs = P(("x", "zl", "core"), b_and_c, None)
    return jax.shard_map(shards, mesh=fine, in_specs=in_specs, out_specs=out_specs, check_vma=False)
```

```python
import functools

import jax
import jax.numpy as jnp
from jax import lax
from jax.experimental import pallas as pl
from jax.experimental.pallas import tpu as pltpu
from jax.sharding import Mesh, PartitionSpec as P

CB = 16
A_ROW = 8
B_DEV = 50
D_DEV = 100
D_ROW = 25
CHUNK = 80
N_DEV = 400
GROUPS = 8
ROWS = A_ROW * B_DEV
KB = 128
TILES = N_DEV // KB
LEFT = N_DEV - TILES * KB
PACKED = 160
SWAP = [(0, 1), (1, 0)]
RANKS_MOST = 9
RANKS_FEW = 3


def count_at_or_above(index, offsets):
    total = jnp.zeros_like(index)
    for k in range(1, 8):
        total = total + jnp.where(index >= offsets[k], 1, 0)
    return total


class Part:
    def __init__(self, table, start):
        self.table, self.start = table, start

    def __getitem__(self, k):
        return self.table[self.start + k]


def parts_of(table):
    return Part(table, 0), Part(table, 8), Part(table, 17), Part(table, 26)


def a_of(row):
    a = jnp.zeros_like(row)
    for k in range(1, A_ROW):
        a = a + jnp.where(row >= k * B_DEV, 1, 0)
    return a


def squeeze_kernel(ranks, table, v_ref, w_ref, by_b):
    place, a_off, v_off, c_off = parts_of(table)
    step = pl.program_id(0)
    b_step = v_ref.shape[0]
    lane = lax.broadcasted_iota(jnp.int32, (D_DEV, KB), 1)
    drow = lax.broadcasted_iota(jnp.int32, (D_DEV, KB), 0)
    base = count_at_or_above(drow + place[1], v_off)
    base = base ^ count_at_or_above((lane >> 4) + place[2] * A_ROW, a_off)
    base = base ^ count_at_or_above(lane & 15, c_off)
    elane = lax.broadcasted_iota(jnp.int32, (ranks * A_ROW, KB), 1)
    erow = lax.broadcasted_iota(jnp.int32, (ranks * A_ROW, KB), 0)
    c = elane & 15
    c_label = count_at_or_above(c, c_off)
    first = jnp.zeros_like(c)
    for k in range(8):
        first = first + jnp.where(c_label == k, c_off[k], 0)
    pick = ((elane >> 4) == (erow & 7)) & ((c - first) == (erow >> 3))
    pick = jnp.where(pick, 1.0, 0.0).astype(jnp.bfloat16)

    @pl.when(step == 0)
    def _():
        by_b[...] = jnp.zeros_like(by_b)

    b0 = place[0] + place[5] * B_DEV + step * b_step
    for p in range(b_step // 2):
        halves = []
        for q in range(2):
            b = 2 * p + q
            b_label = count_at_or_above(b0 + b, v_off)
            x = jnp.where(base == b_label, v_ref[b].astype(jnp.float32), 0.0).astype(jnp.bfloat16)
            halves.append(lax.dot_general(pick, x, (((1,), (1,)), ((), ())), preferred_element_type=jnp.float32))
        for r in range(ranks):
            pair = jnp.concatenate([h[r * A_ROW:(r + 1) * A_ROW] for h in halves], axis=0)
            start = pl.multiple_of(step * (b_step * A_ROW) + 16 * p, 16)
            by_b[r, pl.ds(start, 16), pl.ds(0, D_DEV)] = pair.astype(jnp.bfloat16)

    @pl.when(step == pl.num_programs(0) - 1)
    def _():
        to = lax.broadcasted_iota(jnp.int32, (ROWS, ROWS), 0)
        source = lax.broadcasted_iota(jnp.int32, (ROWS, ROWS), 1)
        a = a_of(to)
        move = jnp.where(source == (to - a * B_DEV) * A_ROW + a, 1.0, 0.0).astype(jnp.bfloat16)
        for r in range(ranks):
            w_ref[r] = jnp.dot(move, by_b[r], preferred_element_type=jnp.float32).astype(jnp.bfloat16)


SMEM = pl.BlockSpec(memory_space=pltpu.SMEM)


def squeeze(ranks, table, v):
    b_step = B_DEV
    return pl.pallas_call(
        functools.partial(squeeze_kernel, ranks),
        grid=(B_DEV // b_step,),
        in_specs=[SMEM, pl.BlockSpec((b_step, D_DEV, KB), lambda i: (i, 0, 0))],
        out_specs=pl.BlockSpec((ranks, ROWS, KB), lambda i: (0, 0, 0)),
        out_shape=jax.ShapeDtypeStruct((ranks, ROWS, KB), jnp.bfloat16),
        scratch_shapes=[pltpu.VMEM((ranks, ROWS, KB), jnp.bfloat16)],
        compiler_params=pltpu.CompilerParams(vmem_limit_bytes=40 * 2**20),
        cost_estimate=pl.CostEstimate(flops=2 * 5000 * 128 * 8 * ranks, bytes_accessed=2400000, transcendentals=0),
        name="squeeze",
    )(table, v)


def pack_kernel(t_ref, out_ref, rows, tail):
    rows[...] = jnp.zeros_like(rows)
    tail[...] = jnp.zeros_like(tail)
    for g in range(GROUPS):
        block = t_ref[0, :, g * N_DEV:(g + 1) * N_DEV].astype(jnp.float32)
        for s in range(TILES):
            rows[pl.ds(g * CHUNK + s * D_ROW, D_ROW), :] = block[:, s * KB:(s + 1) * KB]
        tail[pl.ds(0, D_ROW), pl.ds(0, LEFT)] = block[:, TILES * KB:]
        left = tail[pl.ds(0, 4, stride=8), :]
        for s in range(1, 8):
            left = left + pltpu.roll(tail[pl.ds(s, 4, stride=8), :], LEFT * s, 1)
        rows[pl.ds(g * CHUNK + TILES * D_ROW, 4), :] = left
    out_ref[...] = rows[...].astype(jnp.bfloat16)


def pack(t):
    vmem = pl.BlockSpec(memory_space=pltpu.VMEM)
    return pl.pallas_call(
        pack_kernel,
        in_specs=[vmem],
        out_specs=vmem,
        out_shape=jax.ShapeDtypeStruct((GROUPS * CHUNK, KB), jnp.bfloat16),
        scratch_shapes=[pltpu.VMEM((GROUPS * CHUNK, KB), jnp.float32), pltpu.VMEM((40, KB), jnp.float32)],
        compiler_params=pltpu.CompilerParams(vmem_limit_bytes=8 * 2**20),
        name="pack",
    )(t)


def fill_rows(tp, t, block, tail):
    block[...] = jnp.zeros_like(block)

    @pl.loop(0, CB // 2)
    def _(i):
        for x in range(4):
            start = pl.multiple_of(((i >> 1) * GROUPS + 2 * x + (i & 1)) * CHUNK, 16)
            chunk = t[pl.ds(start, CHUNK), :].astype(jnp.float32)
            for s in range(TILES):
                block[pl.ds(x * D_ROW, D_ROW), pl.ds(s * KB, KB)] = chunk[s * D_ROW:(s + 1) * D_ROW]
            left = chunk[TILES * D_ROW:TILES * D_ROW + 4]
            for s in range(8):
                tail[x, pl.ds(s, 4, stride=8), :] = left if s == 0 else pltpu.roll(left, KB - LEFT * s, 1)
            block[pl.ds(x * D_ROW, D_ROW), pl.ds(TILES * KB, LEFT)] = tail[x, pl.ds(0, D_ROW), pl.ds(0, LEFT)]
        tp[pl.ds(pl.multiple_of(i * KB, KB), KB), :] = block[...].astype(jnp.bfloat16)


def fill_labels(table, base, a_labels):
    place, a_off, v_off, _ = parts_of(table)
    row = lax.broadcasted_iota(jnp.int32, (ROWS, KB), 0)
    lane = lax.broadcasted_iota(jnp.int32, (ROWS, KB), 1)
    a = a_of(row)
    d_label = count_at_or_above(lane + place[1], v_off)
    for s in range(4):
        a_labels[s] = count_at_or_above(a + s * A_ROW, a_off)
    for h in range(2):
        first = place[0] + yn_at(h, table) * 2 * B_DEV
        bd_label = d_label ^ count_at_or_above(row - a * B_DEV + first, v_off)

        @pl.loop(0, 4)
        def _(j):
            base[j, h] = (bd_label ^ a_labels[x_at(2 * j, table)]).astype(jnp.float32).astype(jnp.bfloat16)


def x_at(step, table):
    return (table[2] + (step >> 1)) & 3


def yn_at(step, table):
    return table[7] ^ (step & 1)


def product(table, j, w_ref, yt, tp, base):
    c_off = parts_of(table)[3]
    halves = []
    for h in range(2):
        labels = base[j, h]
        masked = []
        for i in range(CB // 2):
            c = 2 * i + yt
            c_label = count_at_or_above(c, c_off)
            rank = jnp.minimum(c - c_off[c_label], w_ref.shape[2] - 1)
            w = w_ref[j, h, rank]
            hit = labels == c_label.astype(jnp.float32).astype(jnp.bfloat16)
            masked.append(jnp.where(hit, w, jnp.zeros_like(w)))
        halves.append(jnp.concatenate(masked, axis=1))
    return jnp.dot(jnp.concatenate(halves, axis=0), tp[...], preferred_element_type=jnp.float32)


def early_kernel(table, w_ref, t, out_ref, base, tp, block, tail, a_labels):
    fill_rows(tp, t, block, tail)
    fill_labels(table, base, a_labels)

    @pl.loop(0, 4)
    def _(j):
        out_ref[j] = product(table, j, w_ref, table[3], tp, base)


def late_kernel(table, w_ref, t, part_ref, base, mine_ref, other_ref, tp, block, tail, acc, side, packed):
    fill_rows(tp, t, block, tail)
    side[...] = jnp.zeros_like(side)
    packed[...] = jnp.zeros_like(packed)

    @pl.loop(0, 4)
    def _(j):
        acc[...] = part_ref[j] + product(table, j, w_ref, 1 - table[3], tp, base)

        @pl.loop(0, 2)
        def _(h):
            part = acc.at[pl.ds(pl.multiple_of(h * ROWS, 8), ROWS)]
            side[pl.ds(0, ROWS), pl.ds(0, LEFT)] = part[:, TILES * KB:]
            for a in range(A_ROW):
                for s in range(TILES):
                    packed[a, pl.ds(8 + s * B_DEV, B_DEV), :] = part[a * B_DEV:(a + 1) * B_DEV, s * KB:(s + 1) * KB]
                left = side[pl.ds(a * B_DEV, 8, stride=8), :]
                for s in range(1, 8):
                    left = left + pltpu.roll(side[pl.ds(a * B_DEV + s, 8, stride=8), :], LEFT * s, 1)
                packed[a, pl.ds(0, 8), :] = left
            to = 4 * (2 * x_at(2 * j, table) + yn_at(h, table))
            for z in range(4):
                mine_ref[to + z] = packed[2 * z + table[4]].astype(jnp.bfloat16)
                other_ref[to + z] = packed[2 * z + 1 - table[4]].astype(jnp.bfloat16)


SCRATCH = [
    pltpu.VMEM((CB // 2 * KB, N_DEV), jnp.bfloat16),
    pltpu.VMEM((KB, N_DEV), jnp.float32),
    pltpu.VMEM((4, 40, KB), jnp.float32),
]
VMEM = pl.BlockSpec(memory_space=pltpu.VMEM)


def early(table, w, t):
    return pl.pallas_call(
        early_kernel,
        in_specs=[SMEM] + [VMEM] * 2,
        out_specs=[VMEM, VMEM],
        out_shape=[
            jax.ShapeDtypeStruct((4, 2 * ROWS, N_DEV), jnp.float32),
            jax.ShapeDtypeStruct((4, 2, ROWS, KB), jnp.bfloat16),
        ],
        scratch_shapes=SCRATCH + [pltpu.VMEM((4, ROWS, KB), jnp.int32)],
        compiler_params=pltpu.CompilerParams(vmem_limit_bytes=32 * 2**20),
        cost_estimate=pl.CostEstimate(flops=2 * 3200 * 1024 * 400, bytes_accessed=9000000, transcendentals=0),
        name="early",
    )(table, w, t)


def late(table, w, t, partial, base):
    o_shape = jax.ShapeDtypeStruct((4 * GROUPS, PACKED, KB), jnp.bfloat16)
    return pl.pallas_call(
        late_kernel,
        in_specs=[SMEM] + [VMEM] * 4,
        out_specs=[VMEM, VMEM],
        out_shape=[o_shape, o_shape],
        scratch_shapes=SCRATCH + [
            pltpu.VMEM((2 * ROWS, N_DEV), jnp.float32),
            pltpu.VMEM((ROWS + 32, KB), jnp.float32),
            pltpu.VMEM((A_ROW, PACKED, KB), jnp.float32),
        ],
        compiler_params=pltpu.CompilerParams(vmem_limit_bytes=32 * 2**20),
        cost_estimate=pl.CostEstimate(flops=2 * 3200 * 1024 * 400, bytes_accessed=11000000, transcendentals=0),
        name="late",
    )(table, w, t, partial, base)


def add_kernel(in_ref, out_ref, tail, rows):
    for g in range(GROUPS):
        total = in_ref[4 * g].astype(jnp.float32)
        for z in range(1, 4):
            total = total + in_ref[4 * g + z].astype(jnp.float32)
        for t in range(TILES):
            rows[:, pl.ds(g * N_DEV + t * KB, KB)] = total[8 + t * B_DEV:8 + (t + 1) * B_DEV]
        for s in range(8):
            part = total[0:8] if s == 0 else pltpu.roll(total[0:8], KB - LEFT * s, 1)
            tail[pl.ds(s, 8, stride=8), :] = part
        rows[:, pl.ds(g * N_DEV + TILES * KB, LEFT)] = tail[pl.ds(0, B_DEV), pl.ds(0, LEFT)]
    out_ref[0] = rows[...].astype(jnp.bfloat16)


def add_up(parts):
    vmem = pl.BlockSpec(memory_space=pltpu.VMEM)
    return pl.pallas_call(
        add_kernel,
        in_specs=[vmem],
        out_specs=vmem,
        out_shape=jax.ShapeDtypeStruct((1, B_DEV, GROUPS * N_DEV), jnp.bfloat16),
        scratch_shapes=[pltpu.VMEM((72, KB), jnp.float32), pltpu.VMEM((B_DEV, GROUPS * N_DEV), jnp.float32)],
        compiler_params=pltpu.CompilerParams(vmem_limit_bytes=20 * 2**20),
        name="add_up",
    )(parts)


def turn(k):
    return [(i, (i - k) % 4) for i in range(4)]


def around(w):
    return jnp.stack([w] + [lax.ppermute(w, "x", turn(k)) for k in (1, 2, 3)])


def again(table, integrals, w, own, beside, *done):
    w = squeeze(RANKS_MOST, table, integrals)
    w = around(jnp.stack([w, lax.ppermute(w, "yn", SWAP)]))
    return late(table, w, beside, *early(table, w, own))


def finish(table, integrals, w, own, beside, *done):
    return late(table, w, beside, *done)


def shards(integrals, amplitudes, a_offsets, vir_offsets, c_offsets):
    f32, bf16 = jnp.float32, jnp.bfloat16
    x, zh, zl, core = (lax.axis_index(name) for name in ("x", "zh", "zl", "core"))
    yn, yt = lax.axis_index("yn"), lax.axis_index("yt")
    place = [(zh * 4 + yt) * B_DEV, (zl * 2 + core) * D_DEV, x, yt, core, 2 * yn, zl, yn]
    table = jnp.concatenate([jnp.stack(place).astype(jnp.int32), a_offsets, vir_offsets, c_offsets])
    narrow = jnp.max(c_offsets[1:] - c_offsets[:-1]) <= RANKS_FEW
    w = squeeze(RANKS_FEW, table, integrals)
    w_beside = lax.ppermute(w, "yn", SWAP)
    t = lax.all_to_all(pack(amplitudes), ("x", "yn"), 0, 0, tiled=True)
    t, w, w_beside = lax.optimization_barrier((t, w, w_beside))
    w = around(jnp.stack([w, w_beside]))
    own = lax.all_gather(t, "zh", axis=0, tiled=True)
    beside = lax.ppermute(own, "yt", SWAP)
    mine, other = lax.cond(narrow, finish, again, table, integrals, w, own, beside, *early(table, w, own))
    got = lax.ppermute(other, "core", SWAP)
    total = (mine.astype(f32) + got.astype(f32)).astype(bf16)
    return add_up(lax.all_to_all(total, ("x", "yn", "zl"), 0, 0, tiled=True))


def solution(mesh):
    fine = Mesh(mesh.devices.reshape(4, 4, 2, 2, 4, 2), ("x", "zh", "yn", "yt", "zl", "core"))
    b_and_c = ("zh", "yn", "yt")
    in_specs = (P(b_and_c, ("zl", "core"), "x"), P(b_and_c, ("zl", "core", "x"), None), P(), P(), P())
    out_specs = P(("x", "zl", "core"), b_and_c, None)
    return jax.shard_map(shards, mesh=fine, in_specs=in_specs, out_specs=out_specs, check_vma=False)
```

```python
import functools

import jax
import jax.numpy as jnp
from jax import lax
from jax.experimental import pallas as pl
from jax.experimental.pallas import tpu as pltpu
from jax.sharding import Mesh, PartitionSpec as P

CB = 16
A_ROW = 8
B_DEV = 50
D_DEV = 100
D_ROW = 25
CHUNK = 80
N_DEV = 400
GROUPS = 8
ROWS = A_ROW * B_DEV
KB = 128
TILES = N_DEV // KB
LEFT = N_DEV - TILES * KB
PACKED = 160
SWAP = [(0, 1), (1, 0)]
RANKS_MOST = 9
RANKS_FEW = 3


def count_at_or_above(index, offsets):
    total = jnp.zeros_like(index)
    for k in range(1, 8):
        total = total + jnp.where(index >= offsets[k], 1, 0)
    return total


class Part:
    def __init__(self, table, start):
        self.table, self.start = table, start

    def __getitem__(self, k):
        return self.table[self.start + k]


def parts_of(table):
    return Part(table, 0), Part(table, 8), Part(table, 17), Part(table, 26)


def a_of(row):
    a = jnp.zeros_like(row)
    for k in range(1, A_ROW):
        a = a + jnp.where(row >= k * B_DEV, 1, 0)
    return a


def squeeze_kernel(ranks, table, v_ref, w_ref, by_b):
    place, a_off, v_off, c_off = parts_of(table)
    step = pl.program_id(0)
    b_step = v_ref.shape[0]
    lane = lax.broadcasted_iota(jnp.int32, (D_DEV, KB), 1)
    drow = lax.broadcasted_iota(jnp.int32, (D_DEV, KB), 0)
    base = count_at_or_above(drow + place[1], v_off)
    base = base ^ count_at_or_above((lane >> 4) + place[2] * A_ROW, a_off)
    base = base ^ count_at_or_above(lane & 15, c_off)
    elane = lax.broadcasted_iota(jnp.int32, (ranks * A_ROW, KB), 1)
    erow = lax.broadcasted_iota(jnp.int32, (ranks * A_ROW, KB), 0)
    c = elane & 15
    c_label = count_at_or_above(c, c_off)
    first = jnp.zeros_like(c)
    for k in range(8):
        first = first + jnp.where(c_label == k, c_off[k], 0)
    pick = ((elane >> 4) == (erow & 7)) & ((c - first) == (erow >> 3))
    pick = jnp.where(pick, 1.0, 0.0).astype(jnp.bfloat16)

    @pl.when(step == 0)
    def _():
        by_b[...] = jnp.zeros_like(by_b)

    b0 = place[0] + place[5] * B_DEV + step * b_step
    for p in range(b_step // 2):
        halves = []
        for q in range(2):
            b = 2 * p + q
            b_label = count_at_or_above(b0 + b, v_off)
            x = jnp.where(base == b_label, v_ref[b].astype(jnp.float32), 0.0).astype(jnp.bfloat16)
            halves.append(lax.dot_general(pick, x, (((1,), (1,)), ((), ())), preferred_element_type=jnp.float32))
        for r in range(ranks):
            pair = jnp.concatenate([h[r * A_ROW:(r + 1) * A_ROW] for h in halves], axis=0)
            start = pl.multiple_of(step * (b_step * A_ROW) + 16 * p, 16)
            by_b[r, pl.ds(start, 16), pl.ds(0, D_DEV)] = pair.astype(jnp.bfloat16)

    @pl.when(step == pl.num_programs(0) - 1)
    def _():
        to = lax.broadcasted_iota(jnp.int32, (ROWS, ROWS), 0)
        source = lax.broadcasted_iota(jnp.int32, (ROWS, ROWS), 1)
        a = a_of(to)
        move = jnp.where(source == (to - a * B_DEV) * A_ROW + a, 1.0, 0.0).astype(jnp.bfloat16)
        for r in range(ranks):
            w_ref[r] = jnp.dot(move, by_b[r], preferred_element_type=jnp.float32).astype(jnp.bfloat16)


SMEM = pl.BlockSpec(memory_space=pltpu.SMEM)


def squeeze(ranks, table, v):
    b_step = B_DEV
    return pl.pallas_call(
        functools.partial(squeeze_kernel, ranks),
        grid=(B_DEV // b_step,),
        in_specs=[SMEM, pl.BlockSpec((b_step, D_DEV, KB), lambda i: (i, 0, 0))],
        out_specs=pl.BlockSpec((ranks, ROWS, KB), lambda i: (0, 0, 0)),
        out_shape=jax.ShapeDtypeStruct((ranks, ROWS, KB), jnp.bfloat16),
        scratch_shapes=[pltpu.VMEM((ranks, ROWS, KB), jnp.bfloat16)],
        compiler_params=pltpu.CompilerParams(vmem_limit_bytes=16 * 2**20),
        cost_estimate=pl.CostEstimate(flops=2 * 5000 * 128 * 8 * ranks, bytes_accessed=2400000, transcendentals=0),
        name="squeeze",
    )(table, v)


def pack_kernel(t_ref, out_ref, rows, tail):
    rows[...] = jnp.zeros_like(rows)
    tail[...] = jnp.zeros_like(tail)
    for g in range(GROUPS):
        block = t_ref[0, :, g * N_DEV:(g + 1) * N_DEV].astype(jnp.float32)
        for s in range(TILES):
            rows[pl.ds(g * CHUNK + s * D_ROW, D_ROW), :] = block[:, s * KB:(s + 1) * KB]
        tail[pl.ds(0, D_ROW), pl.ds(0, LEFT)] = block[:, TILES * KB:]
        left = tail[pl.ds(0, 4, stride=8), :]
        for s in range(1, 8):
            left = left + pltpu.roll(tail[pl.ds(s, 4, stride=8), :], LEFT * s, 1)
        rows[pl.ds(g * CHUNK + TILES * D_ROW, 4), :] = left
    out_ref[...] = rows[...].astype(jnp.bfloat16)


def pack(t):
    vmem = pl.BlockSpec(memory_space=pltpu.VMEM)
    return pl.pallas_call(
        pack_kernel,
        in_specs=[vmem],
        out_specs=vmem,
        out_shape=jax.ShapeDtypeStruct((GROUPS * CHUNK, KB), jnp.bfloat16),
        scratch_shapes=[pltpu.VMEM((GROUPS * CHUNK, KB), jnp.float32), pltpu.VMEM((40, KB), jnp.float32)],
        compiler_params=pltpu.CompilerParams(vmem_limit_bytes=8 * 2**20),
        name="pack",
    )(t)


def fill_rows(tp, t, block, tail):
    block[...] = jnp.zeros_like(block)

    @pl.loop(0, CB // 2)
    def _(i):
        for x in range(4):
            start = pl.multiple_of(((i >> 1) * GROUPS + 2 * x + (i & 1)) * CHUNK, 16)
            chunk = t[pl.ds(start, CHUNK), :].astype(jnp.float32)
            for s in range(TILES):
                block[pl.ds(x * D_ROW, D_ROW), pl.ds(s * KB, KB)] = chunk[s * D_ROW:(s + 1) * D_ROW]
            left = chunk[TILES * D_ROW:TILES * D_ROW + 4]
            for s in range(8):
                tail[x, pl.ds(s, 4, stride=8), :] = left if s == 0 else pltpu.roll(left, KB - LEFT * s, 1)
            block[pl.ds(x * D_ROW, D_ROW), pl.ds(TILES * KB, LEFT)] = tail[x, pl.ds(0, D_ROW), pl.ds(0, LEFT)]
        tp[pl.ds(pl.multiple_of(i * KB, KB), KB), :] = block[...].astype(jnp.bfloat16)


def fill_labels(table, base, a_labels):
    place, a_off, v_off, _ = parts_of(table)
    row = lax.broadcasted_iota(jnp.int32, (ROWS, KB), 0)
    lane = lax.broadcasted_iota(jnp.int32, (ROWS, KB), 1)
    a = a_of(row)
    d_label = count_at_or_above(lane + place[1], v_off)
    for s in range(4):
        a_labels[s] = count_at_or_above(a + s * A_ROW, a_off)
    for h in range(2):
        first = place[0] + yn_at(h, table) * 2 * B_DEV
        bd_label = d_label ^ count_at_or_above(row - a * B_DEV + first, v_off)

        @pl.loop(0, 4)
        def _(j):
            base[j, h] = (bd_label ^ a_labels[x_at(2 * j, table)]).astype(jnp.float32).astype(jnp.bfloat16)


def x_at(step, table):
    return (table[2] + (step >> 1)) & 3


def yn_at(step, table):
    return table[7] ^ (step & 1)


def product(table, j, w_ref, yt, tp, base):
    c_off = parts_of(table)[3]
    halves = []
    for h in range(2):
        labels = base[j, h]
        masked = []
        for i in range(CB // 2):
            c = 2 * i + yt
            c_label = count_at_or_above(c, c_off)
            rank = jnp.minimum(c - c_off[c_label], w_ref.shape[2] - 1)
            w = w_ref[j, h, rank]
            hit = labels == c_label.astype(jnp.float32).astype(jnp.bfloat16)
            masked.append(jnp.where(hit, w, jnp.zeros_like(w)))
        halves.append(jnp.concatenate(masked, axis=1))
    return jnp.dot(jnp.concatenate(halves, axis=0), tp[...], preferred_element_type=jnp.float32)


def early_kernel(table, w_ref, t, out_ref, base, tp, block, tail, a_labels):
    fill_rows(tp, t, block, tail)
    fill_labels(table, base, a_labels)

    @pl.loop(0, 4)
    def _(j):
        out_ref[j] = product(table, j, w_ref, table[3], tp, base)


def late_kernel(table, w_ref, t, part_ref, base, mine_ref, other_ref, tp, block, tail, acc, side, packed):
    fill_rows(tp, t, block, tail)
    side[...] = jnp.zeros_like(side)
    packed[...] = jnp.zeros_like(packed)

    @pl.loop(0, 4)
    def _(j):
        acc[...] = part_ref[j] + product(table, j, w_ref, 1 - table[3], tp, base)

        @pl.loop(0, 2)
        def _(h):
            part = acc.at[pl.ds(pl.multiple_of(h * ROWS, 8), ROWS)]
            side[pl.ds(0, ROWS), pl.ds(0, LEFT)] = part[:, TILES * KB:]
            for a in range(A_ROW):
                for s in range(TILES):
                    packed[a, pl.ds(8 + s * B_DEV, B_DEV), :] = part[a * B_DEV:(a + 1) * B_DEV, s * KB:(s + 1) * KB]
                left = side[pl.ds(a * B_DEV, 8, stride=8), :]
                for s in range(1, 8):
                    left = left + pltpu.roll(side[pl.ds(a * B_DEV + s, 8, stride=8), :], LEFT * s, 1)
                packed[a, pl.ds(0, 8), :] = left
            to = 4 * (2 * x_at(2 * j, table) + yn_at(h, table))
            for z in range(4):
                mine_ref[to + z] = packed[2 * z + table[4]].astype(jnp.bfloat16)
                other_ref[to + z] = packed[2 * z + 1 - table[4]].astype(jnp.bfloat16)


SCRATCH = [
    pltpu.VMEM((CB // 2 * KB, N_DEV), jnp.bfloat16),
    pltpu.VMEM((KB, N_DEV), jnp.float32),
    pltpu.VMEM((4, 40, KB), jnp.float32),
]
VMEM = pl.BlockSpec(memory_space=pltpu.VMEM)


def early(table, w, t):
    return pl.pallas_call(
        early_kernel,
        in_specs=[SMEM] + [VMEM] * 2,
        out_specs=[VMEM, VMEM],
        out_shape=[
            jax.ShapeDtypeStruct((4, 2 * ROWS, N_DEV), jnp.float32),
            jax.ShapeDtypeStruct((4, 2, ROWS, KB), jnp.bfloat16),
        ],
        scratch_shapes=SCRATCH + [pltpu.VMEM((4, ROWS, KB), jnp.int32)],
        compiler_params=pltpu.CompilerParams(vmem_limit_bytes=16 * 2**20),
        cost_estimate=pl.CostEstimate(flops=2 * 3200 * 1024 * 400, bytes_accessed=9000000, transcendentals=0),
        name="early",
    )(table, w, t)


def late(table, w, t, partial, base):
    o_shape = jax.ShapeDtypeStruct((4 * GROUPS, PACKED, KB), jnp.bfloat16)
    return pl.pallas_call(
        late_kernel,
        in_specs=[SMEM] + [VMEM] * 4,
        out_specs=[VMEM, VMEM],
        out_shape=[o_shape, o_shape],
        scratch_shapes=SCRATCH + [
            pltpu.VMEM((2 * ROWS, N_DEV), jnp.float32),
            pltpu.VMEM((ROWS + 32, KB), jnp.float32),
            pltpu.VMEM((A_ROW, PACKED, KB), jnp.float32),
        ],
        compiler_params=pltpu.CompilerParams(vmem_limit_bytes=16 * 2**20),
        cost_estimate=pl.CostEstimate(flops=2 * 3200 * 1024 * 400, bytes_accessed=11000000, transcendentals=0),
        name="late",
    )(table, w, t, partial, base)


def add_kernel(in_ref, out_ref, tail, rows):
    for g in range(GROUPS):
        total = in_ref[4 * g].astype(jnp.float32)
        for z in range(1, 4):
            total = total + in_ref[4 * g + z].astype(jnp.float32)
        for t in range(TILES):
            rows[:, pl.ds(g * N_DEV + t * KB, KB)] = total[8 + t * B_DEV:8 + (t + 1) * B_DEV]
        for s in range(8):
            part = total[0:8] if s == 0 else pltpu.roll(total[0:8], KB - LEFT * s, 1)
            tail[pl.ds(s, 8, stride=8), :] = part
        rows[:, pl.ds(g * N_DEV + TILES * KB, LEFT)] = tail[pl.ds(0, B_DEV), pl.ds(0, LEFT)]
    out_ref[0] = rows[...].astype(jnp.bfloat16)


def add_up(parts):
    vmem = pl.BlockSpec(memory_space=pltpu.VMEM)
    return pl.pallas_call(
        add_kernel,
        in_specs=[vmem],
        out_specs=vmem,
        out_shape=jax.ShapeDtypeStruct((1, B_DEV, GROUPS * N_DEV), jnp.bfloat16),
        scratch_shapes=[pltpu.VMEM((72, KB), jnp.float32), pltpu.VMEM((B_DEV, GROUPS * N_DEV), jnp.float32)],
        compiler_params=pltpu.CompilerParams(vmem_limit_bytes=20 * 2**20),
        name="add_up",
    )(parts)


def turn(k):
    return [(i, (i - k) % 4) for i in range(4)]


def around(w):
    return jnp.stack([w] + [lax.ppermute(w, "x", turn(k)) for k in (1, 2, 3)])


def again(table, integrals, w, own, beside, *done):
    w = squeeze(RANKS_MOST, table, integrals)
    w = around(jnp.stack([w, lax.ppermute(w, "yn", SWAP)]))
    return late(table, w, beside, *early(table, w, own))


def finish(table, integrals, w, own, beside, *done):
    return late(table, w, beside, *done)


def shards(integrals, amplitudes, a_offsets, vir_offsets, c_offsets):
    f32, bf16 = jnp.float32, jnp.bfloat16
    x, zh, zl, core = (lax.axis_index(name) for name in ("x", "zh", "zl", "core"))
    yn, yt = lax.axis_index("yn"), lax.axis_index("yt")
    place = [(zh * 4 + yt) * B_DEV, (zl * 2 + core) * D_DEV, x, yt, core, 2 * yn, zl, yn]
    table = jnp.concatenate([jnp.stack(place).astype(jnp.int32), a_offsets, vir_offsets, c_offsets])
    narrow = jnp.max(c_offsets[1:] - c_offsets[:-1]) <= RANKS_FEW
    w = squeeze(RANKS_FEW, table, integrals)
    w_beside = lax.ppermute(w, "yn", SWAP)
    t = lax.all_to_all(pack(amplitudes), ("x", "yn"), 0, 0, tiled=True)
    t, w, w_beside = lax.optimization_barrier((t, w, w_beside))
    w = around(jnp.stack([w, w_beside]))
    own = lax.all_gather(t, "zh", axis=0, tiled=True)
    beside = lax.ppermute(own, "yt", SWAP)
    mine, other = lax.cond(narrow, finish, again, table, integrals, w, own, beside, *early(table, w, own))
    got = lax.ppermute(other, "core", SWAP)
    total = (mine.astype(f32) + got.astype(f32)).astype(bf16)
    return add_up(lax.all_to_all(total, ("x", "yn", "zl"), 0, 0, tiled=True))


def solution(mesh):
    fine = Mesh(mesh.devices.reshape(4, 4, 2, 2, 4, 2), ("x", "zh", "yn", "yt", "zl", "core"))
    b_and_c = ("zh", "yn", "yt")
    in_specs = (P(b_and_c, ("zl", "core"), "x"), P(b_and_c, ("zl", "core", "x"), None), P(), P(), P())
    out_specs = P(("x", "zl", "core"), b_and_c, None)
    return jax.shard_map(shards, mesh=fine, in_specs=in_specs, out_specs=out_specs, check_vma=False)
```
